128 devices in a mesh: ox: 32 (over y, x, core), oy: 4 (over z).
Axes of the slice: x: 4, y: 4, z: 4, core: 2. Of those that a mesh axis runs over, the one named last changes fastest.
Arguments:
- state: float32 [4, 16, 32, 4096], P(None, None, 'oy', 'ox'), may hold values from -6 to 6
- levels: int32 [32, 4096], P('oy', 'ox'), may hold values from 0 to 16
- owner: int32 [262144, 1], P(('ox', 'oy')), may hold values from 0 to 127; in each aligned block of 2048 rows (0 to 2047, 2048 to 4095, ...) at most 48 rows name the same one
- atm_cell: int32 [262144], P(('ox', 'oy')), may hold values from 0 to 511
- area: float32 [262144], P(('ox', 'oy')), may hold values from 0.1 to 1
- air_temp: float32 [65536], P(('ox', 'oy')), may hold values from -6 to 6
- exchange_rate: float32 [65536], P(('ox', 'oy')), may hold values from 0.2 to 1
- rainfall: float32 [65536], P(('ox', 'oy')), may hold values from -3 to 3
Outputs:
- next_state: float32 [4, 16, 32, 4096], P(None, None, 'oy', 'ox')
The draws below stay inside these ranges and needn't reach their ends.
Inputs may be any that keep to these rules, and one draw needn't show every extreme that they name: Of the 2048 exchange-grid cells of one device, at most 48 name the same owner.
All inputs are finite; a program needn't handle non-finite values.
Results may differ from the reference program's by a relative error of at most 0.0003.
Values sent between devices are 32-bit elements; how exact they have to be, the bound alone decides.
A program may use at most 64 MiB of HBM per device.

```python
import math
import jax
import jax.numpy as jnp
import numpy as np
from jax import lax

NZ = 16
CY = 8
CX = 128
ATM = 65536
NY = 32
NX = 4096
XG = 2048
A_DEV = 512
CAP = 48
N_OX = 32
N_OY = 4
DEVICES = 128


def plant(drawn, key, low, high):
    shape = drawn.shape
    index_at = [jax.random.randint(jax.random.fold_in(key, axis), (), 0, shape[axis]) for axis in range(len(shape))]
    drawn = drawn.at[tuple(index_at)].set(low)
    longest = shape.index(max(shape))
    index_at[longest] = (index_at[longest] + 1) % shape[longest]
    return drawn.at[tuple(index_at)].set(high)


def steps_of(stream_key, shape, split, least, top_value):
    factor_of, own = 1.0, jax.random.fold_in(stream_key, 6)
    for dim, parts in split:
        steps = jnp.exp(jax.random.uniform(jax.random.fold_in(own, dim), (parts,), jnp.float32, least / len(split), top_value / len(split)))
        factor_of = factor_of * jnp.repeat(steps, shape[dim] // parts).reshape([-1 if axis == dim else 1 for axis in range(len(shape))])
    return factor_of


def assign_block(stream_key, own, number, rows, count, top, reach, slope):
    order = jax.random.permutation(stream_key, count)
    heavy_load, ordinary = shares(count, rows * top, reach, slope, True), shares(count, rows * top, reach, slope, False)
    places = jnp.arange(count)

    def named(tallies, turn):
        used = int((tallies > 0).sum())
        fixed = max(1, used // 4)
        shifted = fixed + (places - fixed + turn * (used - fixed)) % max(1, count - fixed)
        return jnp.zeros((count,), jnp.int32).at[order[jnp.where(places < fixed, places, shifted)]].set(jnp.asarray(tallies, jnp.int32))

    tallies = jnp.where(number % 4 == 0, named(heavy_load, number // 4), named(ordinary, number - number // 4 - 1))
    mixed = jax.random.permutation(jax.random.fold_in(own, 3), count)
    giver, taker = mixed[0:count // 2 * 2:2], mixed[1:count // 2 * 2:2]
    margin = jnp.minimum(tallies[giver] - 1, reach - tallies[taker]) // 2
    margin = jnp.where((giver == order[0]) | (taker == order[0]) | (tallies[taker] == 0), 0, jnp.maximum(margin, 0))
    shifted = jax.random.randint(jax.random.fold_in(own, 4), (count // 2,), 0, 1 << 20) % (margin + 1)
    tallies = tallies.at[giver].add(-shifted).at[taker].add(shifted)
    members = jnp.searchsorted(jnp.cumsum(tallies), jnp.arange(rows * top), side="right").astype(jnp.int32)
    listing = members.reshape(top, rows).T
    listing = listing[jax.random.permutation(jax.random.fold_in(own, 1), rows)]
    turn = jax.random.randint(jax.random.fold_in(own, 2), (rows, 1), 0, top)
    return jnp.take_along_axis(listing, (jnp.arange(top)[None, :] + turn) % top, axis=1)


def shares(count, total, reach, slope, full):
    weights = [(1 << 20) // math.isqrt(grade ** slope) + 1 for grade in range(1, count + 1)]
    largest = reach if full else min(reach, max(-(-total // count), total * weights[0] // sum(weights)))
    least = 1 if total - largest >= count - 1 else 0
    given, rest = [largest] + [least] * (count - 1), total - largest - least * (count - 1)
    while rest > 0:
        free = [i for i in range(1, count) if given[i] < largest] or [i for i in range(1, count) if given[i] < reach]
        pool, budget = sum([weights[i] for i in free]), rest
        for i in free:
            extra = min(reach - given[i], max(1, budget * weights[i] // pool), rest)
            given[i] = given[i] + extra
            rest = rest - extra
    return np.array(given)


def bell_draw(key, extent, scale, most, pieces=(), kind=jnp.bfloat16):
    factor_of = steps_of(key, extent, pieces, -0.22, 0.18) if pieces else 1.0
    entries = jax.random.normal(key, extent, jnp.float32) * scale * factor_of
    return jnp.minimum(jnp.maximum(entries, -most), most).astype(kind)


def setup_inputs(seed: int = 0) -> dict:
    keys = jax.random.split(jax.random.key(seed), 9)
    state = bell_draw(keys[0], (4, NZ, NY, NX), 1.0, 6.0, ((2, 4), (3, 32)), jnp.float32)
    levels = plant(jax.random.randint(keys[1], (NY, NX), 0, NZ + 1), jax.random.fold_in(keys[1], 1), 0, NZ).astype(jnp.int32)
    owner_keys = jax.random.split(jax.random.fold_in(keys[2], 1), (DEVICES * XG) // XG)
    owner_turns = jax.random.permutation(jax.random.fold_in(keys[2], 3), (DEVICES * XG) // XG)
    owner = jax.vmap(lambda own, number: assign_block(jax.random.fold_in(keys[2], 2), own, number, XG, DEVICES, 1, CAP, 2))(owner_keys, owner_turns).reshape((DEVICES * XG, 1))
    atm_cell = plant(jax.random.randint(keys[3], (DEVICES * XG,), 0, A_DEV), jax.random.fold_in(keys[3], 1), 0, A_DEV - 1).astype(jnp.int32)
    area = jnp.clip(jnp.exp(math.log(1.0) - 2.3025851 * jax.random.uniform(keys[4], (DEVICES * XG,), jnp.float32) ** steps_of(keys[4], (DEVICES * XG,), ((0, 128),), -0.2, 0.2)), 0.1, 1.0)
    air_temp = bell_draw(keys[5], (ATM,), 1.0, 6.0, ((0, 128),), jnp.float32)
    exchange_rate = jnp.clip(jnp.exp(math.log(1.0) - 1.609438 * jax.random.uniform(keys[6], (ATM,), jnp.float32) ** steps_of(keys[6], (ATM,), ((0, 128),), -0.2, 0.2)), 0.2, 1.0)
    rainfall = bell_draw(keys[7], (ATM,), 0.5, 3.0, ((0, 128),), jnp.float32)
    return {"state": state, "levels": levels, "owner": owner, "atm_cell": atm_cell, "area": area, "air_temp": air_temp, "exchange_rate": exchange_rate, "rainfall": rainfall}


EDDY_KAPPA = 0.1
VISC = 0.1
STEP = 0.2
SEA_TOP_PLANE = 0.5


def middle_box_entry(field):
    return field[:, 1:-1, 1:-1]


def beside(field):
    return (field[:, 1:-1, 2:], field[:, 1:-1, :-2], field[:, 2:, 1:-1], field[:, :-2, 1:-1])


def distribute_across(field, submerged_indicator):
    middle = middle_box_entry(field)
    summed = jnp.zeros_like(middle)
    for neighbour, wet_near in zip(beside(field), beside(submerged_indicator)):
        summed = summed + wet_near * (neighbour - middle)
    return middle_box_entry(submerged_indicator) * summed


def diapycnal_blend(middle, submerged_halfway):
    empty = jnp.zeros_like(middle[:1])
    beneath = jnp.concatenate([middle[1:], empty], 0)
    overhead = jnp.concatenate([empty, middle[:-1]], 0)
    wet_beneath = jnp.concatenate([submerged_halfway[1:], empty], 0)
    wet_overhead = jnp.concatenate([empty, submerged_halfway[:-1]], 0)
    return submerged_halfway * (wet_beneath * (beneath - middle) + wet_overhead * (overhead - middle))


def gradient(pressure, submerged_indicator, first, second):
    middle = middle_box_entry(pressure)
    near = beside(pressure)
    wet_near = beside(submerged_indicator)
    return 0.5 * (wet_near[first] * (near[first] - middle) + wet_near[second] * (middle - near[second]))


def advance(haloed_grid_array, coriolis, thermal_box, fresh_cell):
    stratum_total = (haloed_grid_array.shape[0] - 1) // 4
    depth_index = lax.broadcasted_iota(jnp.float32, (stratum_total, 1, 1), 0)
    submerged_indicator = (depth_index < haloed_grid_array[4 * stratum_total][None]).astype(jnp.float32)
    thermal_array = haloed_grid_array[0:stratum_total]
    brine_array = haloed_grid_array[stratum_total:2 * stratum_total]
    u_vel = haloed_grid_array[2 * stratum_total:3 * stratum_total]
    v_vel = haloed_grid_array[3 * stratum_total:4 * stratum_total]
    seawater_heaviness = submerged_indicator * (0.8 * brine_array - 0.2 * thermal_array)
    pressure = 0.1 * jnp.cumsum(seawater_heaviness, 0)
    grad_x = gradient(pressure, submerged_indicator, 0, 1)
    grad_y = gradient(pressure, submerged_indicator, 2, 3)
    submerged_halfway = middle_box_entry(submerged_indicator)
    thermal_halfway = middle_box_entry(thermal_array)
    salt_mid = middle_box_entry(brine_array)
    u_mid = middle_box_entry(u_vel)
    v_mid = middle_box_entry(v_vel)
    next_thermal_array = submerged_halfway * (thermal_halfway + EDDY_KAPPA * (distribute_across(thermal_array, submerged_indicator) + diapycnal_blend(thermal_halfway, submerged_halfway)))
    next_thermal_array = next_thermal_array.at[0].add(SEA_TOP_PLANE * submerged_halfway[0] * thermal_box)
    next_brine = submerged_halfway * (salt_mid + EDDY_KAPPA * (distribute_across(brine_array, submerged_indicator) + diapycnal_blend(salt_mid, submerged_halfway)))
    next_brine = next_brine.at[0].add(SEA_TOP_PLANE * submerged_halfway[0] * fresh_cell)
    next_eastward_speed = submerged_halfway * (u_mid + STEP * (coriolis * v_mid - grad_x) + VISC * distribute_across(u_vel, submerged_indicator))
    next_northward_speed = submerged_halfway * (v_mid + STEP * (-coriolis * u_mid - grad_y) + VISC * distribute_across(v_vel, submerged_indicator))
    return jnp.stack([next_thermal_array, next_brine, next_eastward_speed, next_northward_speed], 0)


def blocks(field):
    cut_field = field.reshape(N_OY, CY, N_OX, CX).transpose(2, 0, 1, 3).reshape(-1)
    return jnp.repeat(cut_field, 2)


def unblock(field):
    return field.reshape(N_OX, N_OY, CY, CX).transpose(1, 2, 0, 3).reshape(NY, NX)


def reference(state, levels, owner, atm_cell, area, air_temp, exchange_rate, rainfall):
    wet_top = (levels > 0).astype(jnp.float32)
    weights = area * blocks(wet_top)
    target = owner[:, 0] * A_DEV + atm_cell
    pooled = jnp.stack([weights * blocks(state[0, 0]), weights * blocks(state[1, 0]), weights], 1)
    totals = jax.ops.segment_sum(pooled, target, num_segments=DEVICES * A_DEV)
    divisor = jnp.maximum(totals[:, 2], 1.0)
    heat_flux = exchange_rate * (air_temp - totals[:, 0] / divisor)
    fresh_flux = rainfall * (totals[:, 1] / divisor)
    pair_area = area.reshape(-1, 2)
    area_sum = jnp.sum(pair_area, 1)
    thermal_box = unblock(jnp.sum(pair_area * heat_flux[target].reshape(-1, 2), 1) / area_sum)
    fresh_cell = unblock(jnp.sum(pair_area * fresh_flux[target].reshape(-1, 2), 1) / area_sum)
    stacked = jnp.concatenate([state.reshape(4 * NZ, NY, NX), levels.astype(jnp.float32)[None]], 0)
    parity = jnp.concatenate([jnp.ones((2 * NZ,), jnp.float32), -jnp.ones((2 * NZ,), jnp.float32), jnp.ones((1,), jnp.float32)], 0)
    wrapped = jnp.concatenate([stacked[:, :, -1:], stacked, stacked[:, :, :1]], 2)
    fold_row = jnp.flip(stacked[:, -1, :], 1) * parity[:, None]
    edge_zero = jnp.zeros((4 * NZ + 1, 1), jnp.float32)
    fold_row = jnp.concatenate([edge_zero, fold_row, edge_zero], 1)
    south_row = jnp.zeros((4 * NZ + 1, 1, NX + 2), jnp.float32)
    haloed_grid_array = jnp.concatenate([south_row, wrapped, fold_row[:, None, :]], 1)
    coriolis = 0.2 + 0.8 * jnp.arange(NY, dtype=jnp.float32)[:, None] / NY
    return advance(haloed_grid_array, coriolis, thermal_box, fresh_cell)
```

```python
import jax
import jax.numpy as jnp
from jax import lax
from jax.experimental import pallas as pl
from jax.experimental.pallas import tpu as pltpu
from jax.sharding import PartitionSpec as P

NZ = 16
CY = 8
CX = 128
DEV = 128
N_OY = 4
TILES = 16
HALF = 64
SLOTS = 48
PLANES = 88
EDDY_KAPPA = 0.1
VISC = 0.1
STEP = 0.2
SEA_TOP = 0.5
F32 = jnp.float32
BF16 = jnp.bfloat16
LOGICAL = pl.DeviceIdType.LOGICAL


def hops(mask):
    ring = (0, 1, 2, 1)
    return 4 * (ring[mask & 3] + ring[(mask >> 3) & 3] + ring[(mask >> 5) & 3]) + ((mask >> 2) & 1)


PARTNERS = sorted(range(1, DEV), key=lambda mask: -hops(mask))


def split(value):
    high = value.astype(BF16).astype(F32)
    return high, value - high


def kernel(
    state, levels, owner, cell, area, air, rate, rain,
    out,
    st, lev, raw_own, raw_cell, raw_area, atm,
    z_own, z_cell, z_pos, z_area, z_val,
    chosen, slot_a, slot_b,
    out_slots, in_slots, out_flux, in_flux, flipped,
    rows, left, right,
    pres, north_out, south_out, halo_in, west_out, east_out, side_in,
    local_sem, out_sem, in_sem, halo_out_sem, halo_in_sem,
):
    ox, oy = lax.axis_index("ox"), lax.axis_index("oy")
    me = ox * N_OY + oy
    n_ox = DEV // N_OY

    loads = [
        pltpu.make_async_copy(source, target, local_sem.at[i])
        for i, (source, target) in enumerate(
            (
                (owner, raw_own), (cell, raw_cell), (area, raw_area), (levels, lev), (state, st),
                (air, atm.at[0, 0:4]), (air, atm.at[0, 4:8]),
                (rate, atm.at[1, 0:4]), (rate, atm.at[1, 4:8]),
                (rain, atm.at[2, 0:4]), (rain, atm.at[2, 4:8]),
            )
        )
    ]
    for copy in loads:
        copy.start()
    barrier = pltpu.get_barrier_semaphore()
    for mask in PARTNERS:
        pl.semaphore_signal(barrier, inc=1, device_id=me ^ mask, device_id_type=LOGICAL)
    for copy in loads:
        copy.wait()

    lane = lax.broadcasted_iota(jnp.int32, (8, 128), 1)
    sub = lax.broadcasted_iota(jnp.int32, (8, 128), 0)
    low_half = lane < HALF
    level = lev[...]

    for source, target in ((raw_own, z_own), (raw_cell, z_cell), (raw_area, z_area)):
        even, odd = source[pl.ds(0, 8, stride=2), :], source[pl.ds(1, 8, stride=2), :]
        for c in range(2):
            index = 2 * (lane & (HALF - 1)) + c
            target[pl.ds(8 * c, 8), :] = jnp.where(
                low_half,
                jnp.take_along_axis(even, index, axis=1),
                jnp.take_along_axis(odd, index, axis=1),
            )
    wet_top = (level > 0).astype(F32)
    temp_top, salt_top = st[0:8, :], st[128:136, :]
    for c in range(2):
        part = pl.ds(8 * c, 8)
        weight = z_area[part, :] * wet_top
        for i, value in enumerate(
            (weight * temp_top, weight * salt_top, weight, z_cell[part, :].astype(F32))
        ):
            high, low = split(value)
            z_val[2 * i, part, :] = high
            z_val[2 * i + 1, part, :] = low

    owner_row = lax.broadcasted_iota(jnp.int32, (DEV, 128), 0)

    def mark_owner(t, carry):
        columns = pl.ds(pl.multiple_of(t * 128, 128), 128)
        chosen[:, columns] = jnp.where(z_own[pl.ds(t, 1), :] == owner_row, 1.0, 0.0).astype(BF16)
        return carry

    lax.fori_loop(0, TILES, mark_owner, 0, unroll=4)

    upto = (
        lax.broadcasted_iota(jnp.int32, (256, 256), 0)
        <= lax.broadcasted_iota(jnp.int32, (256, 256), 1)
    )
    upto = jnp.where(upto, 1.0, 0.0).astype(BF16)
    seen = jnp.zeros((DEV, 1), F32)
    for b in range(TILES // 2):
        block = chosen[:, 256 * b : 256 * (b + 1)]
        count = jnp.dot(block, upto, preferred_element_type=F32)
        place = jnp.sum(block.astype(F32) * (count + seen), axis=0, keepdims=True) - 1.0
        z_pos[2 * b : 2 * b + 1, :] = place[:, :128]
        z_pos[2 * b + 1 : 2 * b + 2, :] = place[:, 128:]
        seen = seen + count[:, 255:256]

    slot_row = lax.broadcasted_iota(jnp.int32, (HALF, 128), 0).astype(F32)

    def fill_slots(t, carry):
        columns = pl.ds(pl.multiple_of(t * 128, 128), 128)
        here = z_pos[pl.ds(t, 1), :] == slot_row
        for target, first, second in ((slot_a, 0, 2), (slot_b, 4, 6)):
            for piece in range(2):
                for rows_at, which in ((0, first), (HALF, second)):
                    value = z_val[which + piece, pl.ds(t, 1), :]
                    target[piece, rows_at : rows_at + HALF, columns] = jnp.where(
                        here, value, 0.0
                    ).astype(BF16)
        return carry

    lax.fori_loop(0, TILES, fill_slots, 0, unroll=2)
    for i, source in enumerate((slot_a, slot_b)):
        total = jnp.zeros((DEV, 128), F32)
        for piece in range(2):
            total = total + lax.dot_general(
                chosen[...], source[piece], (((1,), (1,)), ((), ())), preferred_element_type=F32
            )
        out_slots[i] = total

    def add_pressure(k, heavy):
        at = pl.multiple_of(k * 8, 8)
        temp, salt = st[pl.ds(at, 8), :], st[pl.ds(128 + at, 8), :]
        heavy = heavy + jnp.where(k < level, 0.8 * salt - 0.2 * temp, 0.0)
        pres[pl.ds(at, 8), :] = 0.1 * heavy
        return heavy

    lax.fori_loop(0, NZ, add_pressure, jnp.zeros((8, 128), F32), unroll=4)
    level_f = level.astype(F32)
    is_top = oy == N_OY - 1
    backward = 127 - lane
    for i in range(10):
        source, base = (st, 64 * i) if i < 8 else (pres, 64 * (i - 8))
        part = pl.ds(8 * i, 8)
        south_out[part, :] = source[pl.ds(base, 8, stride=8), :]
        top = source[pl.ds(base + 7, 8, stride=8), :]
        mirrored = jnp.take_along_axis(top, backward, axis=1)
        if 4 <= i < 8:
            mirrored = -mirrored
        north_out[part, :] = jnp.where(is_top, mirrored, top)
    top = jnp.broadcast_to(level_f[7:8, :], (8, 128))
    mirrored = jnp.take_along_axis(top, backward, axis=1)
    north_out[80:88, :] = jnp.where(is_top, mirrored, top)
    south_out[80:88, :] = jnp.broadcast_to(level_f[0:1, :], (8, 128))

    def pack_columns(k, packed):
        west, east = packed
        at = pl.multiple_of(k * 8, 8)
        for f in range(5):
            source, base = (st, 128 * f) if f < 4 else (pres, 0)
            plane = source[pl.ds(base + at, 8), :]
            place = 16 * f + k
            west = jnp.where(lane == place, pltpu.roll(plane, place, 1), west)
            east = jnp.where(lane == place, pltpu.roll(plane, place + 1, 1), east)
        return west, east

    none = jnp.zeros((8, 128), F32)
    west, east = lax.fori_loop(0, NZ, pack_columns, (none, none), unroll=2)
    west_out[...] = jnp.where(lane == 80, pltpu.roll(level_f, 80, 1), west)
    east_out[...] = jnp.where(lane == 80, pltpu.roll(level_f, 81, 1), east)

    pl.semaphore_wait(barrier, DEV - 1)
    for mask in PARTNERS:
        partner = me ^ mask
        pltpu.make_async_remote_copy(
            out_slots.at[:, pl.ds(partner, 1)], in_slots.at[:, pl.ds(me, 1)],
            out_sem.at[0], in_sem.at[0], device_id=partner, device_id_type=LOGICAL,
        ).start()
    own_slots = pltpu.make_async_copy(
        out_slots.at[:, pl.ds(me, 1)], in_slots.at[:, pl.ds(me, 1)], local_sem.at[0]
    )
    own_slots.start()

    def halo(source, target, out_at, in_at, device):
        return pltpu.make_async_remote_copy(
            source, target, halo_out_sem.at[out_at], halo_in_sem.at[in_at],
            device_id=device, device_id_type=LOGICAL,
        )

    to_west = halo(west_out, side_in.at[0], 2, 2, lax.rem(ox + n_ox - 1, n_ox) * N_OY + oy)
    to_east = halo(east_out, side_in.at[1], 3, 3, lax.rem(ox + 1, n_ox) * N_OY + oy)
    above = jnp.where(is_top, me ^ (DEV - N_OY), me + 1)
    lands = jnp.where(is_top, 0, 1)
    to_north = halo(north_out, halo_in.at[lands], 0, lands, above)
    to_south = halo(south_out, halo_in.at[0], 1, 0, me - 1)
    to_west.start()
    to_east.start()
    to_north.start()

    @pl.when(oy > 0)
    def _():
        to_south.start()

    def everything(buffers, which):
        source, target = buffers
        if which == 0:
            source, target = source.at[:, pl.ds(0, DEV - 1)], target.at[:, pl.ds(0, DEV - 1)]
        else:
            source, target = source.at[pl.ds(0, DEV - 1)], target.at[pl.ds(0, DEV - 1)]
        return pltpu.make_async_remote_copy(
            source, target, out_sem.at[which], in_sem.at[which],
            device_id=me ^ 1, device_id_type=LOGICAL,
        )

    slots_moved = everything((out_slots, in_slots), 0)
    slots_moved.wait_recv()
    own_slots.wait()

    for i in range(8):
        a, b = pl.ds(8 * i, 8), pl.ds(HALF + 8 * i, 8)
        for plane, first, second in ((0, 0, 2), (1, 4, None)):
            one, two = in_slots[plane, a, :], in_slots[plane, b, :]
            head = jnp.where(low_half, one, pltpu.roll(two, HALF, 1))
            tail = jnp.where(low_half, pltpu.roll(one, HALF, 1), two)
            rows[first, a, :], rows[first + 1, a, :] = split(head)
            if second is not None:
                rows[second, a, :], rows[second + 1, a, :] = split(tail)
            else:
                rows[6, a, :] = tail
    column_row = lax.broadcasted_iota(jnp.int32, (128, 128), 0)

    def mark_cells(r, carry):
        columns = pl.ds(pl.multiple_of(r * 128, 128), 128)
        place = rows[6, pl.ds(r, 1), :].astype(jnp.int32)
        right[:, columns] = jnp.where((place & 127) == column_row, 1.0, 0.0).astype(BF16)
        mine = (place >> 7) == (sub & 3)
        stack = []
        for value in range(3):
            high, low = rows[2 * value, pl.ds(r, 1), :], rows[2 * value + 1, pl.ds(r, 1), :]
            stack.append(jnp.where(mine, jnp.where(sub < 4, high, low), 0.0))
        stack.append(none)
        left[:, columns] = jnp.concatenate(stack, axis=0).astype(BF16)
        return carry

    lax.fori_loop(0, HALF, mark_cells, 0, unroll=4)
    sums = lax.dot_general(
        left[...], right[...], (((1,), (1,)), ((), ())), preferred_element_type=F32
    )
    total_t, total_s, total_w = (
        part + pltpu.roll(part, 4, 0) for part in (sums[0:8], sums[8:16], sums[16:24])
    )
    divisor = jnp.maximum(total_w, 1.0)
    heat_flux = atm[1] * (atm[0] - total_t / divisor)
    fresh_flux = atm[2] * (total_s / divisor)
    for i in range(TILES):
        part = pl.ds(8 * i, 8)
        plane = in_slots[1, part, :]
        place = jnp.where(low_half, pltpu.roll(plane, HALF, 1), plane).astype(jnp.int32)
        column, chunk = place & 127, place >> 7
        picked = none
        for h in range(4):
            heat = jnp.take_along_axis(
                jnp.broadcast_to(heat_flux[h : h + 1, :], (8, 128)), column, axis=1
            )
            fresh = jnp.take_along_axis(
                jnp.broadcast_to(fresh_flux[h : h + 1, :], (8, 128)), column, axis=1
            )
            picked = jnp.where(chunk == h, jnp.where(low_half, heat, fresh), picked)
        out_flux[part, :] = picked

    for mask in PARTNERS:
        partner = me ^ mask
        pltpu.make_async_remote_copy(
            out_flux.at[pl.ds(partner, 1)], in_flux.at[pl.ds(me, 1)],
            out_sem.at[1], in_sem.at[1], device_id=partner, device_id_type=LOGICAL,
        ).start()
    own_flux = pltpu.make_async_copy(
        out_flux.at[pl.ds(me, 1)], in_flux.at[pl.ds(me, 1)], local_sem.at[1]
    )
    own_flux.start()

    halo(west_out, side_in.at[0], 2, 2, me).wait_recv()
    halo(east_out, side_in.at[1], 3, 3, me).wait_recv()
    halo(north_out, halo_in.at[0], 0, 0, me).wait_recv()

    @pl.when(oy > 0)
    def _():
        halo(north_out, halo_in.at[1], 0, 1, me).wait_recv()

    @pl.when(oy == 0)
    def _():
        halo_in[1] = jnp.zeros((PLANES, 128), F32)

    from_east, from_west = side_in[0], side_in[1]

    def around(plane, place):
        return (
            jnp.where(lane == 127, pltpu.roll(from_east, 127 - place, 1), pltpu.roll(plane, 127, 1)),
            jnp.where(lane == 0, pltpu.roll(from_west, 128 - place, 1), pltpu.roll(plane, 1, 1)),
            jnp.where(sub == 7, halo_in[0, pl.ds(place, 1), :], pltpu.roll(plane, 7, 0)),
            jnp.where(sub == 0, halo_in[1, pl.ds(place, 1), :], pltpu.roll(plane, 1, 0)),
        )

    levels_near = around(level_f, 80)
    row_at = (oy * CY + sub).astype(F32)
    coriolis = 0.2 + 0.8 * row_at / (CY * N_OY)

    def step(k, carry):
        depth = k.astype(F32)
        at = pl.multiple_of(k * 8, 8)
        up = pl.multiple_of(jnp.maximum(k - 1, 0) * 8, 8)
        down = pl.multiple_of(jnp.minimum(k + 1, NZ - 1) * 8, 8)
        wet = (depth < level_f).astype(F32)
        wet_near = [(depth < near).astype(F32) for near in levels_near]
        wet_down = jnp.where(k < NZ - 1, (depth + 1.0 < level_f).astype(F32), 0.0)
        wet_up = jnp.where(k > 0, (depth - 1.0 < level_f).astype(F32), 0.0)

        def spread(plane, place):
            total = none
            for near, mask in zip(around(plane, place), wet_near):
                total = total + mask * (near - plane)
            return wet * total

        for f in range(2):
            base = 128 * f
            plane = st[pl.ds(base + at, 8), :]
            over, under = st[pl.ds(base + up, 8), :], st[pl.ds(base + down, 8), :]
            vertical = wet * (wet_down * (under - plane) + wet_up * (over - plane))
            out[pl.ds(base + at, 8), :] = wet * (
                plane + EDDY_KAPPA * (spread(plane, 16 * f + k) + vertical)
            )
        p = pres[pl.ds(at, 8), :]
        p_e, p_w, p_n, p_s = around(p, 64 + k)
        grad_x = 0.5 * (wet_near[0] * (p_e - p) + wet_near[1] * (p - p_w))
        grad_y = 0.5 * (wet_near[2] * (p_n - p) + wet_near[3] * (p - p_s))
        u, v = st[pl.ds(256 + at, 8), :], st[pl.ds(384 + at, 8), :]
        out[pl.ds(256 + at, 8), :] = wet * (
            u + STEP * (coriolis * v - grad_x) + VISC * spread(u, 32 + k)
        )
        out[pl.ds(384 + at, 8), :] = wet * (
            v + STEP * (-coriolis * u - grad_y) + VISC * spread(v, 48 + k)
        )
        return carry

    lax.fori_loop(0, NZ, step, 0, unroll=2)

    flux_moved = everything((out_flux, in_flux), 1)
    flux_moved.wait_recv()
    own_flux.wait()

    flipped[...] = in_flux[...].T
    owners = [z_own[8 * c : 8 * c + 8, :] for c in range(2)]
    places = [z_pos[8 * c : 8 * c + 8, :] for c in range(2)]
    found = [[none, none], [none, none]]
    for s in range(SLOTS):
        for c in range(2):
            here = places[c] == float(s)
            for v in range(2):
                table = jnp.broadcast_to(flipped[HALF * v + s : HALF * v + s + 1, :], (8, 128))
                found[v][c] = jnp.where(
                    here, jnp.take_along_axis(table, owners[c], axis=1), found[v][c]
                )
    area_0, area_1 = z_area[0:8, :], z_area[8:16, :]
    share = SEA_TOP * wet_top / (area_0 + area_1)
    for v in range(2):
        surface = (area_0 * found[v][0] + area_1 * found[v][1]) * share
        out[128 * v : 128 * v + 8, :] = out[128 * v : 128 * v + 8, :] + surface

    slots_moved.wait_send()
    flux_moved.wait_send()
    to_west.wait_send()
    to_east.wait_send()
    to_north.wait_send()

    @pl.when(oy > 0)
    def _():
        to_south.wait_send()


def per_device(state, levels, owner, atm_cell, area, air_temp, exchange_rate, rainfall):
    any_space = pl.BlockSpec(memory_space=pl.ANY)
    result = pl.pallas_call(
        kernel,
        out_shape=jax.ShapeDtypeStruct((4 * NZ * CY, CX), F32),
        in_specs=[any_space] * 8,
        out_specs=pl.BlockSpec(memory_space=pltpu.VMEM),
        scratch_shapes=[
            pltpu.VMEM((512, 128), F32),
            pltpu.VMEM((8, 128), jnp.int32),
            pltpu.VMEM((TILES, 128), jnp.int32),
            pltpu.VMEM((TILES, 128), jnp.int32),
            pltpu.VMEM((TILES, 128), F32),
            pltpu.VMEM((3, 8, 128), F32),
            pltpu.VMEM((TILES, 128), jnp.int32),
            pltpu.VMEM((TILES, 128), jnp.int32),
            pltpu.VMEM((TILES, 128), F32),
            pltpu.VMEM((TILES, 128), F32),
            pltpu.VMEM((8, TILES, 128), F32),
            pltpu.VMEM((DEV, TILES * 128), BF16),
            pltpu.VMEM((2, 128, TILES * 128), BF16),
            pltpu.VMEM((2, 128, TILES * 128), BF16),
            pltpu.VMEM((2, DEV, 128), F32),
            pltpu.VMEM((2, DEV, 128), F32),
            pltpu.VMEM((DEV, 128), F32),
            pltpu.VMEM((DEV, 128), F32),
            pltpu.VMEM((128, 128), F32),
            pltpu.VMEM((7, HALF, 128), F32),
            pltpu.VMEM((32, HALF * 128), BF16),
            pltpu.VMEM((128, HALF * 128), BF16),
            pltpu.VMEM((128, 128), F32),
            pltpu.VMEM((PLANES, 128), F32),
            pltpu.VMEM((PLANES, 128), F32),
            pltpu.VMEM((2, PLANES, 128), F32),
            pltpu.VMEM((8, 128), F32),
            pltpu.VMEM((8, 128), F32),
            pltpu.VMEM((2, 8, 128), F32),
            pltpu.SemaphoreType.DMA((11,)),
            pltpu.SemaphoreType.DMA((2,)),
            pltpu.SemaphoreType.DMA((2,)),
            pltpu.SemaphoreType.DMA((4,)),
            pltpu.SemaphoreType.DMA((4,)),
        ],
        compiler_params=pltpu.CompilerParams(
            collective_id=0, has_side_effects=True, vmem_limit_bytes=60 * 1024 * 1024
        ),
    )(
        state.reshape(4 * NZ * CY, CX),
        levels,
        owner.reshape(TILES, 128),
        atm_cell.reshape(TILES, 128),
        area.reshape(TILES, 128),
        air_temp.reshape(4, 128),
        exchange_rate.reshape(4, 128),
        rainfall.reshape(4, 128),
    )
    return result.reshape(4, NZ, CY, CX)


def solution(mesh):
    entries = P(("ox", "oy"))
    in_specs = (
        P(None, None, "oy", "ox"),
        P("oy", "ox"),
        P(("ox", "oy"), None),
        entries,
        entries,
        entries,
        entries,
        entries,
    )
    return jax.shard_map(
        per_device,
        mesh=mesh,
        in_specs=in_specs,
        out_specs=P(None, None, "oy", "ox"),
        check_vma=False,
    )
```

```python
import jax
import jax.numpy as jnp
from jax import lax
from jax.experimental import pallas as pl
from jax.experimental.pallas import tpu as pltpu
from jax.sharding import PartitionSpec as P

NZ = 16
CY = 8
CX = 128
DEV = 128
N_OY = 4
TILES = 16
HALF = 64
SLOTS = 48
GROUP = 8
PLANES = 88
EDDY_KAPPA = 0.1
VISC = 0.1
STEP = 0.2
SEA_TOP = 0.5
F32 = jnp.float32
BF16 = jnp.bfloat16
LOGICAL = pl.DeviceIdType.LOGICAL


def hops(mask):
    ring = (0, 1, 2, 1)
    return 4 * (ring[mask & 3] + ring[(mask >> 3) & 3] + ring[(mask >> 5) & 3]) + ((mask >> 2) & 1)


PARTNERS = sorted(range(1, DEV), key=lambda mask: -hops(mask))


def split(value):
    high = value.astype(BF16).astype(F32)
    return high, value - high


def kernel(
    state, levels, owner, cell, area, air, rate, rain,
    out,
    st, lev, raw_own, raw_cell, raw_area, atm,
    z_own, z_cell, z_pos, z_area, z_val,
    chosen, slot_a, slot_b,
    out_slots, in_slots, out_flux, in_flux, flipped,
    rows,
    pres, north_out, south_out, halo_in, west_out, east_out, side_in,
    local_sem, out_sem, in_sem, halo_out_sem, halo_in_sem,
):
    ox, oy = lax.axis_index("ox"), lax.axis_index("oy")
    me = ox * N_OY + oy
    n_ox = DEV // N_OY

    loads = [
        pltpu.make_async_copy(source, target, local_sem.at[i])
        for i, (source, target) in enumerate(
            (
                (owner, raw_own), (cell, raw_cell), (area, raw_area), (levels, lev), (state, st),
                (air, atm.at[0, 0:4]), (air, atm.at[0, 4:8]),
                (rate, atm.at[1, 0:4]), (rate, atm.at[1, 4:8]),
                (rain, atm.at[2, 0:4]), (rain, atm.at[2, 4:8]),
            )
        )
    ]
    barrier = pltpu.get_barrier_semaphore()
    for mask in PARTNERS:
        pl.semaphore_signal(barrier, inc=1, device_id=me ^ mask, device_id_type=LOGICAL)
    for copy in loads:
        copy.start()
    for copy in loads:
        copy.wait()

    lane = lax.broadcasted_iota(jnp.int32, (8, 128), 1)
    sub = lax.broadcasted_iota(jnp.int32, (8, 128), 0)
    low_half = lane < HALF
    level = lev[...]

    for source, target in ((raw_own, z_own), (raw_cell, z_cell), (raw_area, z_area)):
        even, odd = source[pl.ds(0, 8, stride=2), :], source[pl.ds(1, 8, stride=2), :]
        for c in range(2):
            index = 2 * (lane & (HALF - 1)) + c
            target[pl.ds(8 * c, 8), :] = jnp.where(
                low_half,
                jnp.take_along_axis(even, index, axis=1),
                jnp.take_along_axis(odd, index, axis=1),
            )
    wet_top = (level > 0).astype(F32)
    temp_top, salt_top = st[0:8, :], st[128:136, :]
    for c in range(2):
        part = pl.ds(8 * c, 8)
        weight = z_area[part, :] * wet_top
        for i, value in enumerate(
            (weight * temp_top, weight * salt_top, weight, z_cell[part, :].astype(F32))
        ):
            high, low = split(value)
            z_val[2 * i, part, :] = high
            z_val[2 * i + 1, part, :] = low

    owner_row = lax.broadcasted_iota(jnp.int32, (DEV, 128), 0)

    def mark_owner(t, carry):
        columns = pl.ds(pl.multiple_of(t * 128, 128), 128)
        chosen[:, columns] = jnp.where(z_own[pl.ds(t, 1), :] == owner_row, 1.0, 0.0).astype(BF16)
        return carry

    lax.fori_loop(0, TILES, mark_owner, 0, unroll=4)

    upto = (
        lax.broadcasted_iota(jnp.int32, (256, 256), 0)
        <= lax.broadcasted_iota(jnp.int32, (256, 256), 1)
    )
    upto = jnp.where(upto, 1.0, 0.0).astype(BF16)
    seen = jnp.zeros((DEV, 1), F32)
    for b in range(TILES // 2):
        block = chosen[:, 256 * b : 256 * (b + 1)]
        count = jnp.dot(block, upto, preferred_element_type=F32)
        place = jnp.sum(block.astype(F32) * (count + seen), axis=0, keepdims=True) - 1.0
        z_pos[2 * b : 2 * b + 1, :] = place[:, :128]
        z_pos[2 * b + 1 : 2 * b + 2, :] = place[:, 128:]
        seen = seen + count[:, 255:256]

    slot_row = lax.broadcasted_iota(jnp.int32, (HALF, 128), 0).astype(F32)

    def fill_slots(t, carry):
        columns = pl.ds(pl.multiple_of(t * 128, 128), 128)
        here = z_pos[pl.ds(t, 1), :] == slot_row
        for target, first, second in ((slot_a, 0, 2), (slot_b, 4, 6)):
            for piece in range(2):
                for rows_at, which in ((0, first), (HALF, second)):
                    value = z_val[which + piece, pl.ds(t, 1), :]
                    target[piece, rows_at : rows_at + HALF, columns] = jnp.where(
                        here, value, 0.0
                    ).astype(BF16)
        return carry

    lax.fori_loop(0, TILES, fill_slots, 0, unroll=2)
    for i, source in enumerate((slot_a, slot_b)):
        total = jnp.zeros((DEV, 128), F32)
        for piece in range(2):
            total = total + lax.dot_general(
                chosen[...], source[piece], (((1,), (1,)), ((), ())), preferred_element_type=F32
            )
        out_slots[i] = total

    pl.semaphore_wait(barrier, DEV - 1)
    for mask in PARTNERS:
        partner = me ^ mask
        pltpu.make_async_remote_copy(
            out_slots.at[:, pl.ds(partner, 1)], in_slots.at[:, pl.ds(me, 1)],
            out_sem.at[0], in_sem.at[0], device_id=partner, device_id_type=LOGICAL,
        ).start()
    own_slots = pltpu.make_async_copy(
        out_slots.at[:, pl.ds(me, 1)], in_slots.at[:, pl.ds(me, 1)], local_sem.at[0]
    )
    own_slots.start()

    def add_pressure(k, heavy):
        at = pl.multiple_of(k * 8, 8)
        temp, salt = st[pl.ds(at, 8), :], st[pl.ds(128 + at, 8), :]
        heavy = heavy + jnp.where(k < level, 0.8 * salt - 0.2 * temp, 0.0)
        pres[pl.ds(at, 8), :] = 0.1 * heavy
        return heavy

    lax.fori_loop(0, NZ, add_pressure, jnp.zeros((8, 128), F32), unroll=4)
    level_f = level.astype(F32)
    is_top = oy == N_OY - 1
    backward = 127 - lane
    for i in range(10):
        source, base = (st, 64 * i) if i < 8 else (pres, 64 * (i - 8))
        part = pl.ds(8 * i, 8)
        south_out[part, :] = source[pl.ds(base, 8, stride=8), :]
        top = source[pl.ds(base + 7, 8, stride=8), :]
        mirrored = jnp.take_along_axis(top, backward, axis=1)
        if 4 <= i < 8:
            mirrored = -mirrored
        north_out[part, :] = jnp.where(is_top, mirrored, top)
    top = jnp.broadcast_to(level_f[7:8, :], (8, 128))
    mirrored = jnp.take_along_axis(top, backward, axis=1)
    north_out[80:88, :] = jnp.where(is_top, mirrored, top)
    south_out[80:88, :] = jnp.broadcast_to(level_f[0:1, :], (8, 128))

    def pack_columns(k, packed):
        west, east = packed
        at = pl.multiple_of(k * 8, 8)
        for f in range(5):
            source, base = (st, 128 * f) if f < 4 else (pres, 0)
            plane = source[pl.ds(base + at, 8), :]
            place = 16 * f + k
            west = jnp.where(lane == place, pltpu.roll(plane, place, 1), west)
            east = jnp.where(lane == place, pltpu.roll(plane, place + 1, 1), east)
        return west, east

    none = jnp.zeros((8, 128), F32)
    west, east = lax.fori_loop(0, NZ, pack_columns, (none, none), unroll=2)
    west_out[...] = jnp.where(lane == 80, pltpu.roll(level_f, 80, 1), west)
    east_out[...] = jnp.where(lane == 80, pltpu.roll(level_f, 81, 1), east)

    def halo(source, target, out_at, in_at, device):
        return pltpu.make_async_remote_copy(
            source, target, halo_out_sem.at[out_at], halo_in_sem.at[in_at],
            device_id=device, device_id_type=LOGICAL,
        )

    to_west = halo(west_out, side_in.at[0], 2, 2, lax.rem(ox + n_ox - 1, n_ox) * N_OY + oy)
    to_east = halo(east_out, side_in.at[1], 3, 3, lax.rem(ox + 1, n_ox) * N_OY + oy)
    above = jnp.where(is_top, me ^ (DEV - N_OY), me + 1)
    lands = jnp.where(is_top, 0, 1)
    to_north = halo(north_out, halo_in.at[lands], 0, lands, above)
    to_south = halo(south_out, halo_in.at[0], 1, 0, me - 1)
    to_west.start()
    to_east.start()
    to_north.start()

    @pl.when(oy > 0)
    def _():
        to_south.start()

    def everything(buffers, which):
        source, target = buffers
        if which == 0:
            source, target = source.at[:, pl.ds(0, DEV - 1)], target.at[:, pl.ds(0, DEV - 1)]
        else:
            source, target = source.at[pl.ds(0, DEV - 1)], target.at[pl.ds(0, DEV - 1)]
        return pltpu.make_async_remote_copy(
            source, target, out_sem.at[which], in_sem.at[which],
            device_id=me ^ 1, device_id_type=LOGICAL,
        )

    slots_moved = everything((out_slots, in_slots), 0)
    slots_moved.wait_recv()
    own_slots.wait()

    for i in range(8):
        a, b = pl.ds(8 * i, 8), pl.ds(HALF + 8 * i, 8)
        for plane, first, second in ((0, 0, 2), (1, 4, None)):
            one, two = in_slots[plane, a, :], in_slots[plane, b, :]
            head = jnp.where(low_half, one, pltpu.roll(two, HALF, 1))
            tail = jnp.where(low_half, pltpu.roll(one, HALF, 1), two)
            rows[first, a, :], rows[first + 1, a, :] = split(head)
            if second is not None:
                rows[second, a, :], rows[second + 1, a, :] = split(tail)
            else:
                rows[6, a, :] = tail
    column_row = lax.broadcasted_iota(jnp.int32, (HALF, 128), 0)
    sums = jnp.zeros((48, HALF), F32)
    for start in range(0, HALF, GROUP):
        lefts, rights = [], []
        for r in range(start, start + GROUP):
            place = rows[6, r : r + 1, :].astype(jnp.int32)
            rights.append(jnp.where((place & 63) == column_row, 1.0, 0.0).astype(BF16))
            mine = (((place >> 7) & 3) + ((place >> 4) & 4)) == sub
            lefts.append(
                jnp.concatenate(
                    [jnp.where(mine, rows[i, r : r + 1, :], 0.0) for i in range(6)], axis=0
                ).astype(BF16)
            )
        sums = sums + lax.dot_general(
            jnp.concatenate(lefts, axis=1),
            jnp.concatenate(rights, axis=1),
            (((1,), (1,)), ((), ())),
            preferred_element_type=F32,
        )
    total_t, total_s, total_w = (
        jnp.concatenate([part, pltpu.roll(part, 4, 0)], axis=1)
        for part in (sums[16 * i : 16 * i + 8] + sums[16 * i + 8 : 16 * i + 16] for i in range(3))
    )
    divisor = jnp.maximum(total_w, 1.0)
    heat_flux = atm[1] * (atm[0] - total_t / divisor)
    fresh_flux = atm[2] * (total_s / divisor)
    for i in range(TILES):
        part = pl.ds(8 * i, 8)
        plane = in_slots[1, part, :]
        place = jnp.where(low_half, pltpu.roll(plane, HALF, 1), plane).astype(jnp.int32)
        column, chunk = place & 127, place >> 7
        picked = none
        for h in range(4):
            heat = jnp.take_along_axis(
                jnp.broadcast_to(heat_flux[h : h + 1, :], (8, 128)), column, axis=1
            )
            fresh = jnp.take_along_axis(
                jnp.broadcast_to(fresh_flux[h : h + 1, :], (8, 128)), column, axis=1
            )
            picked = jnp.where(chunk == h, jnp.where(low_half, heat, fresh), picked)
        out_flux[part, :] = picked

    for mask in PARTNERS:
        partner = me ^ mask
        pltpu.make_async_remote_copy(
            out_flux.at[pl.ds(partner, 1)], in_flux.at[pl.ds(me, 1)],
            out_sem.at[1], in_sem.at[1], device_id=partner, device_id_type=LOGICAL,
        ).start()
    own_flux = pltpu.make_async_copy(
        out_flux.at[pl.ds(me, 1)], in_flux.at[pl.ds(me, 1)], local_sem.at[1]
    )
    own_flux.start()

    halo(west_out, side_in.at[0], 2, 2, me).wait_recv()
    halo(east_out, side_in.at[1], 3, 3, me).wait_recv()
    halo(north_out, halo_in.at[0], 0, 0, me).wait_recv()

    @pl.when(oy > 0)
    def _():
        halo(north_out, halo_in.at[1], 0, 1, me).wait_recv()

    @pl.when(oy == 0)
    def _():
        halo_in[1] = jnp.zeros((PLANES, 128), F32)

    from_east, from_west = side_in[0], side_in[1]

    def around(plane, place):
        return (
            jnp.where(lane == 127, pltpu.roll(from_east, 127 - place, 1), pltpu.roll(plane, 127, 1)),
            jnp.where(lane == 0, pltpu.roll(from_west, 128 - place, 1), pltpu.roll(plane, 1, 1)),
            jnp.where(sub == 7, halo_in[0, pl.ds(place, 1), :], pltpu.roll(plane, 7, 0)),
            jnp.where(sub == 0, halo_in[1, pl.ds(place, 1), :], pltpu.roll(plane, 1, 0)),
        )

    levels_near = around(level_f, 80)
    row_at = (oy * CY + sub).astype(F32)
    coriolis = 0.2 + 0.8 * row_at / (CY * N_OY)

    def step(k, carry):
        depth = k.astype(F32)
        at = pl.multiple_of(k * 8, 8)
        up = pl.multiple_of(jnp.maximum(k - 1, 0) * 8, 8)
        down = pl.multiple_of(jnp.minimum(k + 1, NZ - 1) * 8, 8)
        wet = (depth < level_f).astype(F32)
        wet_near = [(depth < near).astype(F32) for near in levels_near]
        wet_down = jnp.where(k < NZ - 1, (depth + 1.0 < level_f).astype(F32), 0.0)
        wet_up = jnp.where(k > 0, (depth - 1.0 < level_f).astype(F32), 0.0)

        def spread(plane, place):
            total = none
            for near, mask in zip(around(plane, place), wet_near):
                total = total + mask * (near - plane)
            return wet * total

        for f in range(2):
            base = 128 * f
            plane = st[pl.ds(base + at, 8), :]
            over, under = st[pl.ds(base + up, 8), :], st[pl.ds(base + down, 8), :]
            vertical = wet * (wet_down * (under - plane) + wet_up * (over - plane))
            out[pl.ds(base + at, 8), :] = wet * (
                plane + EDDY_KAPPA * (spread(plane, 16 * f + k) + vertical)
            )
        p = pres[pl.ds(at, 8), :]
        p_e, p_w, p_n, p_s = around(p, 64 + k)
        grad_x = 0.5 * (wet_near[0] * (p_e - p) + wet_near[1] * (p - p_w))
        grad_y = 0.5 * (wet_near[2] * (p_n - p) + wet_near[3] * (p - p_s))
        u, v = st[pl.ds(256 + at, 8), :], st[pl.ds(384 + at, 8), :]
        out[pl.ds(256 + at, 8), :] = wet * (
            u + STEP * (coriolis * v - grad_x) + VISC * spread(u, 32 + k)
        )
        out[pl.ds(384 + at, 8), :] = wet * (
            v + STEP * (-coriolis * u - grad_y) + VISC * spread(v, 48 + k)
        )
        return carry

    lax.fori_loop(0, NZ, step, 0, unroll=2)

    flux_moved = everything((out_flux, in_flux), 1)
    flux_moved.wait_recv()
    own_flux.wait()

    flipped[...] = in_flux[...].T
    owners = [z_own[8 * c : 8 * c + 8, :] for c in range(2)]
    places = [z_pos[8 * c : 8 * c + 8, :] for c in range(2)]
    found = [[none, none], [none, none]]
    for s in range(SLOTS):
        for c in range(2):
            here = places[c] == float(s)
            for v in range(2):
                table = jnp.broadcast_to(flipped[HALF * v + s : HALF * v + s + 1, :], (8, 128))
                found[v][c] = jnp.where(
                    here, jnp.take_along_axis(table, owners[c], axis=1), found[v][c]
                )
    area_0, area_1 = z_area[0:8, :], z_area[8:16, :]
    share = SEA_TOP * wet_top / (area_0 + area_1)
    for v in range(2):
        surface = (area_0 * found[v][0] + area_1 * found[v][1]) * share
        out[128 * v : 128 * v + 8, :] = out[128 * v : 128 * v + 8, :] + surface

    slots_moved.wait_send()
    flux_moved.wait_send()
    to_west.wait_send()
    to_east.wait_send()
    to_north.wait_send()

    @pl.when(oy > 0)
    def _():
        to_south.wait_send()


def per_device(state, levels, owner, atm_cell, area, air_temp, exchange_rate, rainfall):
    any_space = pl.BlockSpec(memory_space=pl.ANY)
    result = pl.pallas_call(
        kernel,
        out_shape=pltpu.VMEM((4 * NZ * CY, CX), F32),
        in_specs=[any_space] * 8,
        out_specs=pl.BlockSpec(memory_space=pltpu.VMEM),
        scratch_shapes=[
            pltpu.VMEM((512, 128), F32),
            pltpu.VMEM((8, 128), jnp.int32),
            pltpu.VMEM((TILES, 128), jnp.int32),
            pltpu.VMEM((TILES, 128), jnp.int32),
            pltpu.VMEM((TILES, 128), F32),
            pltpu.VMEM((3, 8, 128), F32),
            pltpu.VMEM((TILES, 128), jnp.int32),
            pltpu.VMEM((TILES, 128), jnp.int32),
            pltpu.VMEM((TILES, 128), F32),
            pltpu.VMEM((TILES, 128), F32),
            pltpu.VMEM((8, TILES, 128), F32),
            pltpu.VMEM((DEV, TILES * 128), BF16),
            pltpu.VMEM((2, 128, TILES * 128), BF16),
            pltpu.VMEM((2, 128, TILES * 128), BF16),
            pltpu.VMEM((2, DEV, 128), F32),
            pltpu.VMEM((2, DEV, 128), F32),
            pltpu.VMEM((DEV, 128), F32),
            pltpu.VMEM((DEV, 128), F32),
            pltpu.VMEM((128, 128), F32),
            pltpu.VMEM((7, HALF, 128), F32),
            pltpu.VMEM((128, 128), F32),
            pltpu.VMEM((PLANES, 128), F32),
            pltpu.VMEM((PLANES, 128), F32),
            pltpu.VMEM((2, PLANES, 128), F32),
            pltpu.VMEM((8, 128), F32),
            pltpu.VMEM((8, 128), F32),
            pltpu.VMEM((2, 8, 128), F32),
            pltpu.SemaphoreType.DMA((11,)),
            pltpu.SemaphoreType.DMA((2,)),
            pltpu.SemaphoreType.DMA((2,)),
            pltpu.SemaphoreType.DMA((4,)),
            pltpu.SemaphoreType.DMA((4,)),
        ],
        compiler_params=pltpu.CompilerParams(
            collective_id=0, has_side_effects=True, vmem_limit_bytes=56 * 1024 * 1024
        ),
    )(
        state.reshape(4 * NZ * CY, CX),
        levels,
        owner.reshape(TILES, 128),
        atm_cell.reshape(TILES, 128),
        area.reshape(TILES, 128),
        air_temp.reshape(4, 128),
        exchange_rate.reshape(4, 128),
        rainfall.reshape(4, 128),
    )
    return result.reshape(4, NZ, CY, CX)


def solution(mesh):
    entries = P(("ox", "oy"))
    in_specs = (
        P(None, None, "oy", "ox"),
        P("oy", "ox"),
        P(("ox", "oy"), None),
        entries,
        entries,
        entries,
        entries,
        entries,
    )
    return jax.shard_map(
        per_device,
        mesh=mesh,
        in_specs=in_specs,
        out_specs=P(None, None, "oy", "ox"),
        check_vma=False,
    )
```

```python
import jax
import jax.numpy as jnp
from jax import lax
from jax.experimental import pallas as pl
from jax.experimental.pallas import tpu as pltpu
from jax.sharding import PartitionSpec as P

NZ = 16
CY = 8
CX = 128
DEV = 128
N_OY = 4
TILES = 16
HALF = 64
SLOTS = 48
GROUP = 8
PLANES = 88
EDDY_KAPPA = 0.1
VISC = 0.1
STEP = 0.2
SEA_TOP = 0.5
F32 = jnp.float32
BF16 = jnp.bfloat16
LOGICAL = pl.DeviceIdType.LOGICAL


def hops(mask):
    ring = (0, 1, 2, 1)
    return 4 * (ring[mask & 3] + ring[(mask >> 3) & 3] + ring[(mask >> 5) & 3]) + ((mask >> 2) & 1)


PARTNERS = sorted(range(1, DEV), key=lambda mask: -(hops(mask) // 4))
SENDS = sorted(range(DEV - 1, 0, -1), key=lambda mask: -(hops(mask) // 4))
RETURNS = sorted(range(DEV - 1, 0, -1), key=lambda mask: -(hops(mask) // 4))


def split(value):
    high = value.astype(BF16).astype(F32)
    return high, value - high


def kernel(
    state, levels, owner, cell, area, air, rate, rain,
    out,
    st, lev, raw_own, raw_cell, raw_area, atm,
    z_own, z_cell, z_pos, z_area, z_val,
    chosen, slot_a, slot_b,
    out_slots, in_slots, out_flux, in_flux, flipped,
    rows,
    pres, north_out, south_out, halo_in, west_out, east_out, side_in,
    local_sem, out_sem, in_sem, halo_out_sem, halo_in_sem,
):
    ox, oy = lax.axis_index("ox"), lax.axis_index("oy")
    me = ox * N_OY + oy
    n_ox = DEV // N_OY

    loads = [
        pltpu.make_async_copy(source, target, local_sem.at[i])
        for i, (source, target) in enumerate(
            (
                (owner, raw_own), (cell, raw_cell), (area, raw_area), (levels, lev), (state, st),
                (air, atm.at[0, 0:4]), (air, atm.at[0, 4:8]),
                (rate, atm.at[1, 0:4]), (rate, atm.at[1, 4:8]),
                (rain, atm.at[2, 0:4]), (rain, atm.at[2, 4:8]),
            )
        )
    ]
    barrier = pltpu.get_barrier_semaphore()
    for mask in PARTNERS:
        pl.semaphore_signal(barrier, inc=1, device_id=me ^ mask, device_id_type=LOGICAL)
    for copy in loads:
        copy.start()
    for copy in loads:
        copy.wait()

    lane = lax.broadcasted_iota(jnp.int32, (8, 128), 1)
    sub = lax.broadcasted_iota(jnp.int32, (8, 128), 0)
    low_half = lane < HALF
    level = lev[...]

    for source, target in ((raw_own, z_own), (raw_cell, z_cell), (raw_area, z_area)):
        even, odd = source[pl.ds(0, 8, stride=2), :], source[pl.ds(1, 8, stride=2), :]
        for c in range(2):
            index = 2 * (lane & (HALF - 1)) + c
            target[pl.ds(8 * c, 8), :] = jnp.where(
                low_half,
                jnp.take_along_axis(even, index, axis=1),
                jnp.take_along_axis(odd, index, axis=1),
            )
    wet_top = (level > 0).astype(F32)
    temp_top, salt_top = st[0:8, :], st[128:136, :]
    for c in range(2):
        part = pl.ds(8 * c, 8)
        weight = z_area[part, :] * wet_top
        for i, value in enumerate(
            (weight * temp_top, weight * salt_top, weight, z_cell[part, :].astype(F32))
        ):
            high, low = split(value)
            z_val[2 * i, part, :] = high
            z_val[2 * i + 1, part, :] = low

    owner_row = lax.broadcasted_iota(jnp.int32, (DEV, 128), 0)

    def mark_owner(t, carry):
        columns = pl.ds(pl.multiple_of(t * 128, 128), 128)
        chosen[:, columns] = jnp.where(z_own[pl.ds(t, 1), :] == owner_row, 1.0, 0.0).astype(BF16)
        return carry

    lax.fori_loop(0, TILES, mark_owner, 0, unroll=4)

    upto = (
        lax.broadcasted_iota(jnp.int32, (256, 256), 0)
        <= lax.broadcasted_iota(jnp.int32, (256, 256), 1)
    )
    upto = jnp.where(upto, 1.0, 0.0).astype(BF16)
    seen = jnp.zeros((DEV, 1), F32)
    for b in range(TILES // 2):
        block = chosen[:, 256 * b : 256 * (b + 1)]
        count = jnp.dot(block, upto, preferred_element_type=F32)
        place = jnp.sum(block.astype(F32) * (count + seen), axis=0, keepdims=True) - 1.0
        z_pos[2 * b : 2 * b + 1, :] = place[:, :128]
        z_pos[2 * b + 1 : 2 * b + 2, :] = place[:, 128:]
        seen = seen + count[:, 255:256]

    slot_row = lax.broadcasted_iota(jnp.int32, (HALF, 128), 0).astype(F32)

    def fill_slots(t, carry):
        columns = pl.ds(pl.multiple_of(t * 128, 128), 128)
        here = z_pos[pl.ds(t, 1), :] == slot_row
        for target, first, second in ((slot_a, 0, 2), (slot_b, 4, 6)):
            for piece in range(2):
                for rows_at, which in ((0, first), (HALF, second)):
                    value = z_val[which + piece, pl.ds(t, 1), :]
                    target[piece, rows_at : rows_at + HALF, columns] = jnp.where(
                        here, value, 0.0
                    ).astype(BF16)
        return carry

    lax.fori_loop(0, TILES, fill_slots, 0, unroll=2)
    for i, source in enumerate((slot_a, slot_b)):
        total = jnp.zeros((DEV, 128), F32)
        for piece in range(2):
            total = total + lax.dot_general(
                chosen[...], source[piece], (((1,), (1,)), ((), ())), preferred_element_type=F32
            )
        out_slots[i] = total

    pl.semaphore_wait(barrier, DEV - 1)
    for mask in SENDS:
        partner = me ^ mask
        pltpu.make_async_remote_copy(
            out_slots.at[:, pl.ds(partner, 1)], in_slots.at[:, pl.ds(me, 1)],
            out_sem.at[0], in_sem.at[0], device_id=partner, device_id_type=LOGICAL,
        ).start()
    own_slots = pltpu.make_async_copy(
        out_slots.at[:, pl.ds(me, 1)], in_slots.at[:, pl.ds(me, 1)], local_sem.at[0]
    )
    own_slots.start()

    def add_pressure(k, heavy):
        at = pl.multiple_of(k * 8, 8)
        temp, salt = st[pl.ds(at, 8), :], st[pl.ds(128 + at, 8), :]
        heavy = heavy + jnp.where(k < level, 0.8 * salt - 0.2 * temp, 0.0)
        pres[pl.ds(at, 8), :] = 0.1 * heavy
        return heavy

    lax.fori_loop(0, NZ, add_pressure, jnp.zeros((8, 128), F32), unroll=4)
    level_f = level.astype(F32)
    is_top = oy == N_OY - 1
    backward = 127 - lane
    for i in range(10):
        source, base = (st, 64 * i) if i < 8 else (pres, 64 * (i - 8))
        part = pl.ds(8 * i, 8)
        south_out[part, :] = source[pl.ds(base, 8, stride=8), :]
        top = source[pl.ds(base + 7, 8, stride=8), :]
        mirrored = jnp.take_along_axis(top, backward, axis=1)
        if 4 <= i < 8:
            mirrored = -mirrored
        north_out[part, :] = jnp.where(is_top, mirrored, top)
    top = jnp.broadcast_to(level_f[7:8, :], (8, 128))
    mirrored = jnp.take_along_axis(top, backward, axis=1)
    north_out[80:88, :] = jnp.where(is_top, mirrored, top)
    south_out[80:88, :] = jnp.broadcast_to(level_f[0:1, :], (8, 128))

    def pack_columns(k, packed):
        west, east = packed
        at = pl.multiple_of(k * 8, 8)
        for f in range(5):
            source, base = (st, 128 * f) if f < 4 else (pres, 0)
            plane = source[pl.ds(base + at, 8), :]
            place = 16 * f + k
            west = jnp.where(lane == place, pltpu.roll(plane, place, 1), west)
            east = jnp.where(lane == place, pltpu.roll(plane, place + 1, 1), east)
        return west, east

    none = jnp.zeros((8, 128), F32)
    west, east = lax.fori_loop(0, NZ, pack_columns, (none, none), unroll=2)
    west_out[...] = jnp.where(lane == 80, pltpu.roll(level_f, 80, 1), west)
    east_out[...] = jnp.where(lane == 80, pltpu.roll(level_f, 81, 1), east)

    def halo(source, target, out_at, in_at, device):
        return pltpu.make_async_remote_copy(
            source, target, halo_out_sem.at[out_at], halo_in_sem.at[in_at],
            device_id=device, device_id_type=LOGICAL,
        )

    to_west = halo(west_out, side_in.at[0], 2, 2, lax.rem(ox + n_ox - 1, n_ox) * N_OY + oy)
    to_east = halo(east_out, side_in.at[1], 3, 3, lax.rem(ox + 1, n_ox) * N_OY + oy)
    above = jnp.where(is_top, me ^ (DEV - N_OY), me + 1)
    lands = jnp.where(is_top, 0, 1)
    to_north = halo(north_out, halo_in.at[lands], 0, lands, above)
    to_south = halo(south_out, halo_in.at[0], 1, 0, me - 1)
    to_west.start()
    to_east.start()
    to_north.start()

    @pl.when(oy > 0)
    def _():
        to_south.start()

    def everything(buffers, which):
        source, target = buffers
        if which == 0:
            source, target = source.at[:, pl.ds(0, DEV - 1)], target.at[:, pl.ds(0, DEV - 1)]
        else:
            source, target = source.at[pl.ds(0, DEV - 1)], target.at[pl.ds(0, DEV - 1)]
        return pltpu.make_async_remote_copy(
            source, target, out_sem.at[which], in_sem.at[which],
            device_id=me ^ 1, device_id_type=LOGICAL,
        )

    slots_moved = everything((out_slots, in_slots), 0)
    slots_moved.wait_recv()
    own_slots.wait()

    for i in range(8):
        a, b = pl.ds(8 * i, 8), pl.ds(HALF + 8 * i, 8)
        for plane, first, second in ((0, 0, 2), (1, 4, None)):
            one, two = in_slots[plane, a, :], in_slots[plane, b, :]
            head = jnp.where(low_half, one, pltpu.roll(two, HALF, 1))
            tail = jnp.where(low_half, pltpu.roll(one, HALF, 1), two)
            rows[first, a, :], rows[first + 1, a, :] = split(head)
            if second is not None:
                rows[second, a, :], rows[second + 1, a, :] = split(tail)
            else:
                rows[6, a, :] = tail
    column_row = lax.broadcasted_iota(jnp.int32, (HALF, 128), 0)
    sums = jnp.zeros((48, HALF), F32)
    for start in range(0, HALF, GROUP):
        lefts, rights = [], []
        for r in range(start, start + GROUP):
            place = rows[6, r : r + 1, :].astype(jnp.int32)
            rights.append(jnp.where((place & 63) == column_row, 1.0, 0.0).astype(BF16))
            mine = (((place >> 7) & 3) + ((place >> 4) & 4)) == sub
            lefts.append(
                jnp.concatenate(
                    [jnp.where(mine, rows[i, r : r + 1, :], 0.0) for i in range(6)], axis=0
                ).astype(BF16)
            )
        sums = sums + lax.dot_general(
            jnp.concatenate(lefts, axis=1),
            jnp.concatenate(rights, axis=1),
            (((1,), (1,)), ((), ())),
            preferred_element_type=F32,
        )
    total_t, total_s, total_w = (
        jnp.concatenate([part, pltpu.roll(part, 4, 0)], axis=1)
        for part in (sums[16 * i : 16 * i + 8] + sums[16 * i + 8 : 16 * i + 16] for i in range(3))
    )
    divisor = jnp.maximum(total_w, 1.0)
    heat_flux = atm[1] * (atm[0] - total_t / divisor)
    fresh_flux = atm[2] * (total_s / divisor)
    for i in range(TILES):
        part = pl.ds(8 * i, 8)
        plane = in_slots[1, part, :]
        place = jnp.where(low_half, pltpu.roll(plane, HALF, 1), plane).astype(jnp.int32)
        column, chunk = place & 127, place >> 7
        picked = none
        for h in range(4):
            heat = jnp.take_along_axis(
                jnp.broadcast_to(heat_flux[h : h + 1, :], (8, 128)), column, axis=1
            )
            fresh = jnp.take_along_axis(
                jnp.broadcast_to(fresh_flux[h : h + 1, :], (8, 128)), column, axis=1
            )
            picked = jnp.where(chunk == h, jnp.where(low_half, heat, fresh), picked)
        out_flux[part, :] = picked

    for mask in RETURNS:
        partner = me ^ mask
        pltpu.make_async_remote_copy(
            out_flux.at[pl.ds(partner, 1)], in_flux.at[pl.ds(me, 1)],
            out_sem.at[1], in_sem.at[1], device_id=partner, device_id_type=LOGICAL,
        ).start()
    own_flux = pltpu.make_async_copy(
        out_flux.at[pl.ds(me, 1)], in_flux.at[pl.ds(me, 1)], local_sem.at[1]
    )
    own_flux.start()

    halo(west_out, side_in.at[0], 2, 2, me).wait_recv()
    halo(east_out, side_in.at[1], 3, 3, me).wait_recv()
    halo(north_out, halo_in.at[0], 0, 0, me).wait_recv()

    @pl.when(oy > 0)
    def _():
        halo(north_out, halo_in.at[1], 0, 1, me).wait_recv()

    @pl.when(oy == 0)
    def _():
        halo_in[1] = jnp.zeros((PLANES, 128), F32)

    from_east, from_west = side_in[0], side_in[1]

    def around(plane, place):
        return (
            jnp.where(lane == 127, pltpu.roll(from_east, 127 - place, 1), pltpu.roll(plane, 127, 1)),
            jnp.where(lane == 0, pltpu.roll(from_west, 128 - place, 1), pltpu.roll(plane, 1, 1)),
            jnp.where(sub == 7, halo_in[0, pl.ds(place, 1), :], pltpu.roll(plane, 7, 0)),
            jnp.where(sub == 0, halo_in[1, pl.ds(place, 1), :], pltpu.roll(plane, 1, 0)),
        )

    levels_near = around(level_f, 80)
    row_at = (oy * CY + sub).astype(F32)
    coriolis = 0.2 + 0.8 * row_at / (CY * N_OY)

    def step(k, carry):
        depth = k.astype(F32)
        at = pl.multiple_of(k * 8, 8)
        up = pl.multiple_of(jnp.maximum(k - 1, 0) * 8, 8)
        down = pl.multiple_of(jnp.minimum(k + 1, NZ - 1) * 8, 8)
        wet = (depth < level_f).astype(F32)
        wet_near = [(depth < near).astype(F32) for near in levels_near]
        wet_down = jnp.where(k < NZ - 1, (depth + 1.0 < level_f).astype(F32), 0.0)
        wet_up = jnp.where(k > 0, (depth - 1.0 < level_f).astype(F32), 0.0)

        def spread(plane, place):
            total = none
            for near, mask in zip(around(plane, place), wet_near):
                total = total + mask * (near - plane)
            return wet * total

        for f in range(2):
            base = 128 * f
            plane = st[pl.ds(base + at, 8), :]
            over, under = st[pl.ds(base + up, 8), :], st[pl.ds(base + down, 8), :]
            vertical = wet * (wet_down * (under - plane) + wet_up * (over - plane))
            out[pl.ds(base + at, 8), :] = wet * (
                plane + EDDY_KAPPA * (spread(plane, 16 * f + k) + vertical)
            )
        p = pres[pl.ds(at, 8), :]
        p_e, p_w, p_n, p_s = around(p, 64 + k)
        grad_x = 0.5 * (wet_near[0] * (p_e - p) + wet_near[1] * (p - p_w))
        grad_y = 0.5 * (wet_near[2] * (p_n - p) + wet_near[3] * (p - p_s))
        u, v = st[pl.ds(256 + at, 8), :], st[pl.ds(384 + at, 8), :]
        out[pl.ds(256 + at, 8), :] = wet * (
            u + STEP * (coriolis * v - grad_x) + VISC * spread(u, 32 + k)
        )
        out[pl.ds(384 + at, 8), :] = wet * (
            v + STEP * (-coriolis * u - grad_y) + VISC * spread(v, 48 + k)
        )
        return carry

    lax.fori_loop(0, NZ, step, 0, unroll=2)

    flux_moved = everything((out_flux, in_flux), 1)
    flux_moved.wait_recv()
    own_flux.wait()

    flipped[...] = in_flux[...].T
    owners = [z_own[8 * c : 8 * c + 8, :] for c in range(2)]
    places = [z_pos[8 * c : 8 * c + 8, :] for c in range(2)]
    found = [[none, none], [none, none]]
    pieces = []
    for v in (1,):
        high, low = split(flipped[HALF * v : HALF * v + SLOTS, :])
        pieces += [high.astype(BF16), low.astype(BF16)]
    pieces = jnp.concatenate(pieces, axis=0)
    slot_at = lax.broadcasted_iota(jnp.int32, (SLOTS, 128), 0).astype(F32)
    for b in range(TILES // 2):
        near = jnp.dot(pieces, chosen[:, 256 * b : 256 * (b + 1)], preferred_element_type=F32)
        for half in range(2):
            t = 2 * b + half
            here = z_pos[t : t + 1, :] == slot_at
            columns = slice(128 * half, 128 * (half + 1))
            for i, v in enumerate((1,)):
                at = 2 * SLOTS * i
                both = near[at : at + SLOTS, columns] + near[at + SLOTS : at + 2 * SLOTS, columns]
                z_val[v, t : t + 1, :] = jnp.sum(
                    jnp.where(here, both, 0.0), axis=0, keepdims=True
                )
    for s in range(SLOTS):
        for c in range(2):
            here = places[c] == float(s)
            for v in (0,):
                table = jnp.broadcast_to(flipped[HALF * v + s : HALF * v + s + 1, :], (8, 128))
                found[v][c] = jnp.where(
                    here, jnp.take_along_axis(table, owners[c], axis=1), found[v][c]
                )
    for v in (1,):
        found[v] = [z_val[v, 8 * c : 8 * c + 8, :] for c in range(2)]
    area_0, area_1 = z_area[0:8, :], z_area[8:16, :]
    share = SEA_TOP * wet_top / (area_0 + area_1)
    for v in range(2):
        surface = (area_0 * found[v][0] + area_1 * found[v][1]) * share
        out[128 * v : 128 * v + 8, :] = out[128 * v : 128 * v + 8, :] + surface

    slots_moved.wait_send()
    flux_moved.wait_send()
    to_west.wait_send()
    to_east.wait_send()
    to_north.wait_send()

    @pl.when(oy > 0)
    def _():
        to_south.wait_send()


def per_device(state, levels, owner, atm_cell, area, air_temp, exchange_rate, rainfall):
    any_space = pl.BlockSpec(memory_space=pl.ANY)
    result = pl.pallas_call(
        kernel,
        out_shape=pltpu.VMEM((4 * NZ * CY, CX), F32),
        in_specs=[any_space] * 8,
        out_specs=pl.BlockSpec(memory_space=pltpu.VMEM),
        scratch_shapes=[
            pltpu.VMEM((512, 128), F32),
            pltpu.VMEM((8, 128), jnp.int32),
            pltpu.VMEM((TILES, 128), jnp.int32),
            pltpu.VMEM((TILES, 128), jnp.int32),
            pltpu.VMEM((TILES, 128), F32),
            pltpu.VMEM((3, 8, 128), F32),
            pltpu.VMEM((TILES, 128), jnp.int32),
            pltpu.VMEM((TILES, 128), jnp.int32),
            pltpu.VMEM((TILES, 128), F32),
            pltpu.VMEM((TILES, 128), F32),
            pltpu.VMEM((8, TILES, 128), F32),
            pltpu.VMEM((DEV, TILES * 128), BF16),
            pltpu.VMEM((2, 128, TILES * 128), BF16),
            pltpu.VMEM((2, 128, TILES * 128), BF16),
            pltpu.VMEM((2, DEV, 128), F32),
            pltpu.VMEM((2, DEV, 128), F32),
            pltpu.VMEM((DEV, 128), F32),
            pltpu.VMEM((DEV, 128), F32),
            pltpu.VMEM((128, 128), F32),
            pltpu.VMEM((7, HALF, 128), F32),
            pltpu.VMEM((128, 128), F32),
            pltpu.VMEM((PLANES, 128), F32),
            pltpu.VMEM((PLANES, 128), F32),
            pltpu.VMEM((2, PLANES, 128), F32),
            pltpu.VMEM((8, 128), F32),
            pltpu.VMEM((8, 128), F32),
            pltpu.VMEM((2, 8, 128), F32),
            pltpu.SemaphoreType.DMA((11,)),
            pltpu.SemaphoreType.DMA((2,)),
            pltpu.SemaphoreType.DMA((2,)),
            pltpu.SemaphoreType.DMA((4,)),
            pltpu.SemaphoreType.DMA((4,)),
        ],
        compiler_params=pltpu.CompilerParams(
            collective_id=0, has_side_effects=True, vmem_limit_bytes=56 * 1024 * 1024
        ),
    )(
        state.reshape(4 * NZ * CY, CX),
        levels,
        owner.reshape(TILES, 128),
        atm_cell.reshape(TILES, 128),
        area.reshape(TILES, 128),
        air_temp.reshape(4, 128),
        exchange_rate.reshape(4, 128),
        rainfall.reshape(4, 128),
    )
    return result.reshape(4, NZ, CY, CX)


def solution(mesh):
    entries = P(("ox", "oy"))
    in_specs = (
        P(None, None, "oy", "ox"),
        P("oy", "ox"),
        P(("ox", "oy"), None),
        entries,
        entries,
        entries,
        entries,
        entries,
    )
    return jax.shard_map(
        per_device,
        mesh=mesh,
        in_specs=in_specs,
        out_specs=P(None, None, "oy", "ox"),
        check_vma=False,
    )
```

```python
import jax
import jax.numpy as jnp
from jax import lax
from jax.experimental import pallas as pl
from jax.experimental.pallas import tpu as pltpu
from jax.sharding import PartitionSpec as P

NZ = 16
CY = 8
CX = 128
DEV = 128
N_OY = 4
TILES = 16
HALF = 64
SLOTS = 48
GROUP = 8
PLANES = 88
EDDY_KAPPA = 0.1
VISC = 0.1
STEP = 0.2
SEA_TOP = 0.5
F32 = jnp.float32
BF16 = jnp.bfloat16
LOGICAL = pl.DeviceIdType.LOGICAL


def hops(mask):
    ring = (0, 1, 2, 1)
    return 4 * (ring[mask & 3] + ring[(mask >> 3) & 3] + ring[(mask >> 5) & 3]) + ((mask >> 2) & 1)


PARTNERS = sorted(range(1, DEV), key=lambda mask: -(hops(mask) // 4))
SENDS = sorted(range(DEV - 1, 0, -1), key=lambda mask: -(hops(mask) // 4))
RETURNS = sorted(range(DEV - 1, 0, -1), key=lambda mask: -(hops(mask) // 4))


def split(value):
    high = value.astype(BF16).astype(F32)
    return high, value - high


def kernel(
    state, levels, owner, cell, area, air, rate, rain,
    out,
    st, lev, raw_own, raw_cell, raw_area, atm,
    z_own, z_cell, z_pos, z_area, z_val,
    chosen, slot_a, slot_b,
    out_slots, in_slots, out_flux, in_flux, flipped,
    rows,
    pres, north_out, south_out, halo_in, west_out, east_out, side_in,
    local_sem, out_sem, in_sem, halo_out_sem, halo_in_sem,
):
    ox, oy = lax.axis_index("ox"), lax.axis_index("oy")
    me = ox * N_OY + oy
    n_ox = DEV // N_OY

    loads = [
        pltpu.make_async_copy(source, target, local_sem.at[i])
        for i, (source, target) in enumerate(
            (
                (owner, raw_own), (cell, raw_cell), (area, raw_area), (levels, lev), (state, st),
                (air, atm.at[0, 0:4]), (air, atm.at[0, 4:8]),
                (rate, atm.at[1, 0:4]), (rate, atm.at[1, 4:8]),
                (rain, atm.at[2, 0:4]), (rain, atm.at[2, 4:8]),
            )
        )
    ]
    barrier = pltpu.get_barrier_semaphore()
    for mask in PARTNERS[:44]:
        pl.semaphore_signal(barrier, inc=1, device_id=me ^ mask, device_id_type=LOGICAL)
    for copy in loads:
        copy.start()
    for mask in PARTNERS[44:]:
        pl.semaphore_signal(barrier, inc=1, device_id=me ^ mask, device_id_type=LOGICAL)
    for copy in loads:
        copy.wait()

    lane = lax.broadcasted_iota(jnp.int32, (8, 128), 1)
    sub = lax.broadcasted_iota(jnp.int32, (8, 128), 0)
    low_half = lane < HALF
    level = lev[...]

    for source, target in ((raw_own, z_own), (raw_cell, z_cell), (raw_area, z_area)):
        even, odd = source[pl.ds(0, 8, stride=2), :], source[pl.ds(1, 8, stride=2), :]
        for c in range(2):
            index = 2 * (lane & (HALF - 1)) + c
            target[pl.ds(8 * c, 8), :] = jnp.where(
                low_half,
                jnp.take_along_axis(even, index, axis=1),
                jnp.take_along_axis(odd, index, axis=1),
            )
    wet_top = (level > 0).astype(F32)
    temp_top, salt_top = st[0:8, :], st[128:136, :]
    for c in range(2):
        part = pl.ds(8 * c, 8)
        weight = z_area[part, :] * wet_top
        for i, value in enumerate(
            (weight * temp_top, weight * salt_top, weight, z_cell[part, :].astype(F32))
        ):
            high, low = split(value)
            z_val[2 * i, part, :] = high
            z_val[2 * i + 1, part, :] = low

    owner_row = lax.broadcasted_iota(jnp.int32, (DEV, 128), 0)

    def mark_owner(t, carry):
        columns = pl.ds(pl.multiple_of(t * 128, 128), 128)
        chosen[:, columns] = jnp.where(z_own[pl.ds(t, 1), :] == owner_row, 1.0, 0.0).astype(BF16)
        return carry

    lax.fori_loop(0, TILES, mark_owner, 0, unroll=4)

    upto = (
        lax.broadcasted_iota(jnp.int32, (256, 256), 0)
        <= lax.broadcasted_iota(jnp.int32, (256, 256), 1)
    )
    upto = jnp.where(upto, 1.0, 0.0).astype(BF16)
    seen = jnp.zeros((DEV, 1), F32)
    for b in range(TILES // 2):
        block = chosen[:, 256 * b : 256 * (b + 1)]
        count = jnp.dot(block, upto, preferred_element_type=F32)
        place = jnp.sum(block.astype(F32) * (count + seen), axis=0, keepdims=True) - 1.0
        z_pos[2 * b : 2 * b + 1, :] = place[:, :128]
        z_pos[2 * b + 1 : 2 * b + 2, :] = place[:, 128:]
        seen = seen + count[:, 255:256]

    slot_row = lax.broadcasted_iota(jnp.int32, (HALF, 128), 0).astype(F32)

    def fill_slots(t, carry):
        columns = pl.ds(pl.multiple_of(t * 128, 128), 128)
        here = z_pos[pl.ds(t, 1), :] == slot_row
        for target, first, second in ((slot_a, 0, 2), (slot_b, 4, 6)):
            for piece in range(2):
                for rows_at, which in ((0, first), (HALF, second)):
                    value = z_val[which + piece, pl.ds(t, 1), :]
                    target[piece, rows_at : rows_at + HALF, columns] = jnp.where(
                        here, value, 0.0
                    ).astype(BF16)
        return carry

    lax.fori_loop(0, TILES, fill_slots, 0, unroll=2)
    for i, source in enumerate((slot_a, slot_b)):
        total = jnp.zeros((DEV, 128), F32)
        for piece in range(2):
            total = total + lax.dot_general(
                chosen[...], source[piece], (((1,), (1,)), ((), ())), preferred_element_type=F32
            )
        out_slots[i] = total

    pl.semaphore_wait(barrier, DEV - 1)
    for mask in SENDS:
        partner = me ^ mask
        pltpu.make_async_remote_copy(
            out_slots.at[:, pl.ds(partner, 1)], in_slots.at[:, pl.ds(me, 1)],
            out_sem.at[0], in_sem.at[0], device_id=partner, device_id_type=LOGICAL,
        ).start()
    own_slots = pltpu.make_async_copy(
        out_slots.at[:, pl.ds(me, 1)], in_slots.at[:, pl.ds(me, 1)], local_sem.at[0]
    )
    own_slots.start()

    def add_pressure(k, heavy):
        at = pl.multiple_of(k * 8, 8)
        temp, salt = st[pl.ds(at, 8), :], st[pl.ds(128 + at, 8), :]
        heavy = heavy + jnp.where(k < level, 0.8 * salt - 0.2 * temp, 0.0)
        pres[pl.ds(at, 8), :] = 0.1 * heavy
        return heavy

    lax.fori_loop(0, NZ, add_pressure, jnp.zeros((8, 128), F32), unroll=4)
    level_f = level.astype(F32)
    is_top = oy == N_OY - 1
    backward = 127 - lane
    for i in range(10):
        source, base = (st, 64 * i) if i < 8 else (pres, 64 * (i - 8))
        part = pl.ds(8 * i, 8)
        south_out[part, :] = source[pl.ds(base, 8, stride=8), :]
        top = source[pl.ds(base + 7, 8, stride=8), :]
        mirrored = jnp.take_along_axis(top, backward, axis=1)
        if 4 <= i < 8:
            mirrored = -mirrored
        north_out[part, :] = jnp.where(is_top, mirrored, top)
    top = jnp.broadcast_to(level_f[7:8, :], (8, 128))
    mirrored = jnp.take_along_axis(top, backward, axis=1)
    north_out[80:88, :] = jnp.where(is_top, mirrored, top)
    south_out[80:88, :] = jnp.broadcast_to(level_f[0:1, :], (8, 128))

    def pack_columns(k, packed):
        west, east = packed
        at = pl.multiple_of(k * 8, 8)
        for f in range(5):
            source, base = (st, 128 * f) if f < 4 else (pres, 0)
            plane = source[pl.ds(base + at, 8), :]
            place = 16 * f + k
            west = jnp.where(lane == place, pltpu.roll(plane, place, 1), west)
            east = jnp.where(lane == place, pltpu.roll(plane, place + 1, 1), east)
        return west, east

    none = jnp.zeros((8, 128), F32)
    west, east = lax.fori_loop(0, NZ, pack_columns, (none, none), unroll=2)
    west_out[...] = jnp.where(lane == 80, pltpu.roll(level_f, 80, 1), west)
    east_out[...] = jnp.where(lane == 80, pltpu.roll(level_f, 81, 1), east)

    def halo(source, target, out_at, in_at, device):
        return pltpu.make_async_remote_copy(
            source, target, halo_out_sem.at[out_at], halo_in_sem.at[in_at],
            device_id=device, device_id_type=LOGICAL,
        )

    to_west = halo(west_out, side_in.at[0], 2, 2, lax.rem(ox + n_ox - 1, n_ox) * N_OY + oy)
    to_east = halo(east_out, side_in.at[1], 3, 3, lax.rem(ox + 1, n_ox) * N_OY + oy)
    above = jnp.where(is_top, me ^ (DEV - N_OY), me + 1)
    lands = jnp.where(is_top, 0, 1)
    to_north = halo(north_out, halo_in.at[lands], 0, lands, above)
    to_south = halo(south_out, halo_in.at[0], 1, 0, me - 1)
    to_west.start()
    to_east.start()
    to_north.start()

    @pl.when(oy > 0)
    def _():
        to_south.start()

    def everything(buffers, which):
        source, target = buffers
        if which == 0:
            source, target = source.at[:, pl.ds(0, DEV - 1)], target.at[:, pl.ds(0, DEV - 1)]
        else:
            source, target = source.at[pl.ds(0, DEV - 1)], target.at[pl.ds(0, DEV - 1)]
        return pltpu.make_async_remote_copy(
            source, target, out_sem.at[which], in_sem.at[which],
            device_id=me ^ 1, device_id_type=LOGICAL,
        )

    slots_moved = everything((out_slots, in_slots), 0)
    slots_moved.wait_recv()
    own_slots.wait()

    for i in range(8):
        a, b = pl.ds(8 * i, 8), pl.ds(HALF + 8 * i, 8)
        for plane, first, second in ((0, 0, 2), (1, 4, None)):
            one, two = in_slots[plane, a, :], in_slots[plane, b, :]
            head = jnp.where(low_half, one, pltpu.roll(two, HALF, 1))
            tail = jnp.where(low_half, pltpu.roll(one, HALF, 1), two)
            rows[first, a, :], rows[first + 1, a, :] = split(head)
            if second is not None:
                rows[second, a, :], rows[second + 1, a, :] = split(tail)
            else:
                rows[6, a, :] = tail
    column_row = lax.broadcasted_iota(jnp.int32, (HALF, 128), 0)
    sums = jnp.zeros((48, HALF), F32)
    for start in range(0, HALF, GROUP):
        lefts, rights = [], []
        for r in range(start, start + GROUP):
            place = rows[6, r : r + 1, :].astype(jnp.int32)
            rights.append(jnp.where((place & 63) == column_row, 1.0, 0.0).astype(BF16))
            mine = (((place >> 7) & 3) + ((place >> 4) & 4)) == sub
            lefts.append(
                jnp.concatenate(
                    [jnp.where(mine, rows[i, r : r + 1, :], 0.0) for i in range(6)], axis=0
                ).astype(BF16)
            )
        sums = sums + lax.dot_general(
            jnp.concatenate(lefts, axis=1),
            jnp.concatenate(rights, axis=1),
            (((1,), (1,)), ((), ())),
            preferred_element_type=F32,
        )
    total_t, total_s, total_w = (
        jnp.concatenate([part, pltpu.roll(part, 4, 0)], axis=1)
        for part in (sums[16 * i : 16 * i + 8] + sums[16 * i + 8 : 16 * i + 16] for i in range(3))
    )
    divisor = jnp.maximum(total_w, 1.0)
    heat_flux = atm[1] * (atm[0] - total_t / divisor)
    fresh_flux = atm[2] * (total_s / divisor)
    for i in range(TILES // 2):
        a, b = pl.ds(8 * i, 8), pl.ds(HALF + 8 * i, 8)
        place = rows[6, a, :].astype(jnp.int32)
        column, chunk = place & 127, place >> 7
        heat, fresh = none, none
        for h in range(4):
            here = chunk == h
            table = jnp.broadcast_to(heat_flux[h : h + 1, :], (8, 128))
            heat = jnp.where(here, jnp.take_along_axis(table, column, axis=1), heat)
            table = jnp.broadcast_to(fresh_flux[h : h + 1, :], (8, 128))
            fresh = jnp.where(here, jnp.take_along_axis(table, column, axis=1), fresh)
        out_flux[a, :] = jnp.where(low_half, heat, pltpu.roll(fresh, HALF, 1))
        out_flux[b, :] = jnp.where(low_half, pltpu.roll(heat, HALF, 1), fresh)

    for mask in RETURNS:
        partner = me ^ mask
        pltpu.make_async_remote_copy(
            out_flux.at[pl.ds(partner, 1)], in_flux.at[pl.ds(me, 1)],
            out_sem.at[1], in_sem.at[1], device_id=partner, device_id_type=LOGICAL,
        ).start()
    own_flux = pltpu.make_async_copy(
        out_flux.at[pl.ds(me, 1)], in_flux.at[pl.ds(me, 1)], local_sem.at[1]
    )
    own_flux.start()

    halo(west_out, side_in.at[0], 2, 2, me).wait_recv()
    halo(east_out, side_in.at[1], 3, 3, me).wait_recv()
    halo(north_out, halo_in.at[0], 0, 0, me).wait_recv()

    @pl.when(oy > 0)
    def _():
        halo(north_out, halo_in.at[1], 0, 1, me).wait_recv()

    @pl.when(oy == 0)
    def _():
        halo_in[1] = jnp.zeros((PLANES, 128), F32)

    from_east, from_west = side_in[0], side_in[1]

    def around(plane, place):
        return (
            jnp.where(lane == 127, pltpu.roll(from_east, 127 - place, 1), pltpu.roll(plane, 127, 1)),
            jnp.where(lane == 0, pltpu.roll(from_west, (128 - place) & 127, 1), pltpu.roll(plane, 1, 1)),
            jnp.where(sub == 7, halo_in[0, pl.ds(place, 1), :], pltpu.roll(plane, 7, 0)),
            jnp.where(sub == 0, halo_in[1, pl.ds(place, 1), :], pltpu.roll(plane, 1, 0)),
        )

    levels_near = around(level_f, 80)
    row_at = (oy * CY + sub).astype(F32)
    coriolis = 0.2 + 0.8 * row_at / (CY * N_OY)

    def step(k, carry):
        depth = k.astype(F32)
        at = pl.multiple_of(k * 8, 8)
        up = pl.multiple_of(jnp.maximum(k - 1, 0) * 8, 8)
        down = pl.multiple_of(jnp.minimum(k + 1, NZ - 1) * 8, 8)
        wet = (depth < level_f).astype(F32)
        wet_near = [(depth < near).astype(F32) for near in levels_near]
        wet_down = jnp.where(k < NZ - 1, (depth + 1.0 < level_f).astype(F32), 0.0)
        wet_up = jnp.where(k > 0, (depth - 1.0 < level_f).astype(F32), 0.0)

        def spread(plane, place):
            total = none
            for near, mask in zip(around(plane, place), wet_near):
                total = total + mask * (near - plane)
            return wet * total

        for f in range(2):
            base = 128 * f
            plane = st[pl.ds(base + at, 8), :]
            over, under = st[pl.ds(base + up, 8), :], st[pl.ds(base + down, 8), :]
            vertical = wet * (wet_down * (under - plane) + wet_up * (over - plane))
            out[pl.ds(base + at, 8), :] = wet * (
                plane + EDDY_KAPPA * (spread(plane, 16 * f + k) + vertical)
            )
        p = pres[pl.ds(at, 8), :]
        p_e, p_w, p_n, p_s = around(p, 64 + k)
        grad_x = 0.5 * (wet_near[0] * (p_e - p) + wet_near[1] * (p - p_w))
        grad_y = 0.5 * (wet_near[2] * (p_n - p) + wet_near[3] * (p - p_s))
        u, v = st[pl.ds(256 + at, 8), :], st[pl.ds(384 + at, 8), :]
        out[pl.ds(256 + at, 8), :] = wet * (
            u + STEP * (coriolis * v - grad_x) + VISC * spread(u, 32 + k)
        )
        out[pl.ds(384 + at, 8), :] = wet * (
            v + STEP * (-coriolis * u - grad_y) + VISC * spread(v, 48 + k)
        )
        return carry

    lax.fori_loop(0, NZ, step, 0, unroll=2)

    flux_moved = everything((out_flux, in_flux), 1)
    flux_moved.wait_recv()
    own_flux.wait()

    flipped[...] = in_flux[...].T
    owners = [z_own[8 * c : 8 * c + 8, :] for c in range(2)]
    places = [z_pos[8 * c : 8 * c + 8, :] for c in range(2)]
    found = [[none, none], [none, none]]
    pieces = []
    for v in (1,):
        high, low = split(flipped[HALF * v : HALF * v + SLOTS, :])
        pieces += [high.astype(BF16), low.astype(BF16)]
    pieces = jnp.concatenate(pieces, axis=0)
    slot_at = lax.broadcasted_iota(jnp.int32, (SLOTS, 128), 0).astype(F32)
    for b in range(TILES // 2):
        near = jnp.dot(pieces, chosen[:, 256 * b : 256 * (b + 1)], preferred_element_type=F32)
        for half in range(2):
            t = 2 * b + half
            here = z_pos[t : t + 1, :] == slot_at
            columns = slice(128 * half, 128 * (half + 1))
            for i, v in enumerate((1,)):
                at = 2 * SLOTS * i
                both = near[at : at + SLOTS, columns] + near[at + SLOTS : at + 2 * SLOTS, columns]
                z_val[v, t : t + 1, :] = jnp.sum(
                    jnp.where(here, both, 0.0), axis=0, keepdims=True
                )
    for s in range(SLOTS):
        for c in range(2):
            here = places[c] == float(s)
            for v in (0,):
                table = jnp.broadcast_to(flipped[HALF * v + s : HALF * v + s + 1, :], (8, 128))
                found[v][c] = jnp.where(
                    here, jnp.take_along_axis(table, owners[c], axis=1), found[v][c]
                )
    for v in (1,):
        found[v] = [z_val[v, 8 * c : 8 * c + 8, :] for c in range(2)]
    area_0, area_1 = z_area[0:8, :], z_area[8:16, :]
    share = SEA_TOP * wet_top / (area_0 + area_1)
    for v in range(2):
        surface = (area_0 * found[v][0] + area_1 * found[v][1]) * share
        out[128 * v : 128 * v + 8, :] = out[128 * v : 128 * v + 8, :] + surface

    slots_moved.wait_send()
    flux_moved.wait_send()
    to_west.wait_send()
    to_east.wait_send()
    to_north.wait_send()

    @pl.when(oy > 0)
    def _():
        to_south.wait_send()


def per_device(state, levels, owner, atm_cell, area, air_temp, exchange_rate, rainfall):
    any_space = pl.BlockSpec(memory_space=pl.ANY)
    result = pl.pallas_call(
        kernel,
        out_shape=pltpu.VMEM((4 * NZ * CY, CX), F32),
        in_specs=[any_space] * 8,
        out_specs=pl.BlockSpec(memory_space=pltpu.VMEM),
        scratch_shapes=[
            pltpu.VMEM((512, 128), F32),
            pltpu.VMEM((8, 128), jnp.int32),
            pltpu.VMEM((TILES, 128), jnp.int32),
            pltpu.VMEM((TILES, 128), jnp.int32),
            pltpu.VMEM((TILES, 128), F32),
            pltpu.VMEM((3, 8, 128), F32),
            pltpu.VMEM((TILES, 128), jnp.int32),
            pltpu.VMEM((TILES, 128), jnp.int32),
            pltpu.VMEM((TILES, 128), F32),
            pltpu.VMEM((TILES, 128), F32),
            pltpu.VMEM((8, TILES, 128), F32),
            pltpu.VMEM((DEV, TILES * 128), BF16),
            pltpu.VMEM((2, 128, TILES * 128), BF16),
            pltpu.VMEM((2, 128, TILES * 128), BF16),
            pltpu.VMEM((2, DEV, 128), F32),
            pltpu.VMEM((2, DEV, 128), F32),
            pltpu.VMEM((DEV, 128), F32),
            pltpu.VMEM((DEV, 128), F32),
            pltpu.VMEM((128, 128), F32),
            pltpu.VMEM((7, HALF, 128), F32),
            pltpu.VMEM((128, 128), F32),
            pltpu.VMEM((PLANES, 128), F32),
            pltpu.VMEM((PLANES, 128), F32),
            pltpu.VMEM((2, PLANES, 128), F32),
            pltpu.VMEM((8, 128), F32),
            pltpu.VMEM((8, 128), F32),
            pltpu.VMEM((2, 8, 128), F32),
            pltpu.SemaphoreType.DMA((11,)),
            pltpu.SemaphoreType.DMA((2,)),
            pltpu.SemaphoreType.DMA((2,)),
            pltpu.SemaphoreType.DMA((4,)),
            pltpu.SemaphoreType.DMA((4,)),
        ],
        compiler_params=pltpu.CompilerParams(
            collective_id=0, has_side_effects=True, vmem_limit_bytes=56 * 1024 * 1024
        ),
    )(
        state.reshape(4 * NZ * CY, CX),
        levels,
        owner.reshape(TILES, 128),
        atm_cell.reshape(TILES, 128),
        area.reshape(TILES, 128),
        air_temp.reshape(4, 128),
        exchange_rate.reshape(4, 128),
        rainfall.reshape(4, 128),
    )
    return result.reshape(4, NZ, CY, CX)


def solution(mesh):
    entries = P(("ox", "oy"))
    in_specs = (
        P(None, None, "oy", "ox"),
        P("oy", "ox"),
        P(("ox", "oy"), None),
        entries,
        entries,
        entries,
        entries,
        entries,
    )
    return jax.shard_map(
        per_device,
        mesh=mesh,
        in_specs=in_specs,
        out_specs=P(None, None, "oy", "ox"),
        check_vma=False,
    )
```

```python
import jax
import jax.numpy as jnp
from jax import lax
from jax.experimental import pallas as pl
from jax.experimental.pallas import tpu as pltpu
from jax.sharding import PartitionSpec as P

NZ = 16
CY = 8
CX = 128
DEV = 128
N_OY = 4
TILES = 16
HALF = 64
SLOTS = 48
GROUP = 8
PLANES = 88
EDDY_KAPPA = 0.1
VISC = 0.1
STEP = 0.2
SEA_TOP = 0.5
F32 = jnp.float32
BF16 = jnp.bfloat16
LOGICAL = pl.DeviceIdType.LOGICAL


def hops(mask):
    ring = (0, 1, 2, 1)
    return 4 * (ring[mask & 3] + ring[(mask >> 3) & 3] + ring[(mask >> 5) & 3]) + ((mask >> 2) & 1)


PARTNERS = sorted(range(1, DEV), key=lambda mask: -(hops(mask) // 4))
SENDS = sorted(range(DEV - 1, 0, -1), key=lambda mask: -(hops(mask) // 4))
RETURNS = sorted(range(DEV - 1, 0, -1), key=lambda mask: -(hops(mask) // 4))


def split(value):
    high = value.astype(BF16).astype(F32)
    return high, value - high


def kernel(
    state, levels, owner, cell, area, air, rate, rain,
    out,
    st, lev, raw_own, raw_cell, raw_area, atm,
    z_own, z_cell, z_pos, z_area, z_val,
    chosen, slot_a, slot_b,
    out_slots, in_slots, out_flux, in_flux, flipped,
    rows,
    pres, north_out, south_out, halo_in, west_out, east_out, side_in,
    local_sem, out_sem, in_sem, halo_out_sem, halo_in_sem,
):
    ox, oy = lax.axis_index("ox"), lax.axis_index("oy")
    me = ox * N_OY + oy
    n_ox = DEV // N_OY

    loads = [
        pltpu.make_async_copy(source, target, local_sem.at[i])
        for i, (source, target) in enumerate(
            (
                (owner, raw_own), (cell, raw_cell), (area, raw_area), (levels, lev), (state, st),
                (air, atm.at[0, 0:4]), (air, atm.at[0, 4:8]),
                (rate, atm.at[1, 0:4]), (rate, atm.at[1, 4:8]),
                (rain, atm.at[2, 0:4]), (rain, atm.at[2, 4:8]),
            )
        )
    ]
    barrier = pltpu.get_barrier_semaphore()
    for mask in PARTNERS[:44]:
        pl.semaphore_signal(barrier, inc=1, device_id=me ^ mask, device_id_type=LOGICAL)
    for copy in loads:
        copy.start()
    for mask in PARTNERS[44:]:
        pl.semaphore_signal(barrier, inc=1, device_id=me ^ mask, device_id_type=LOGICAL)
    for copy in loads:
        copy.wait()

    lane = lax.broadcasted_iota(jnp.int32, (8, 128), 1)
    sub = lax.broadcasted_iota(jnp.int32, (8, 128), 0)
    low_half = lane < HALF
    level = lev[...]

    for source, target in ((raw_own, z_own), (raw_cell, z_cell), (raw_area, z_area)):
        even, odd = source[pl.ds(0, 8, stride=2), :], source[pl.ds(1, 8, stride=2), :]
        for c in range(2):
            index = 2 * (lane & (HALF - 1)) + c
            target[pl.ds(8 * c, 8), :] = jnp.where(
                low_half,
                jnp.take_along_axis(even, index, axis=1),
                jnp.take_along_axis(odd, index, axis=1),
            )
    wet_top = (level > 0).astype(F32)
    temp_top, salt_top = st[0:8, :], st[128:136, :]
    for c in range(2):
        part = pl.ds(8 * c, 8)
        weight = z_area[part, :] * wet_top
        for i, value in enumerate(
            (weight * temp_top, weight * salt_top, weight, z_cell[part, :].astype(F32))
        ):
            high, low = split(value)
            z_val[2 * i, part, :] = high
            z_val[2 * i + 1, part, :] = low

    owner_row = lax.broadcasted_iota(jnp.int32, (DEV, 128), 0)

    def mark_owner(t, carry):
        columns = pl.ds(pl.multiple_of(t * 128, 128), 128)
        chosen[:, columns] = jnp.where(z_own[pl.ds(t, 1), :] == owner_row, 1.0, 0.0).astype(BF16)
        return carry

    lax.fori_loop(0, TILES, mark_owner, 0, unroll=4)

    upto = (
        lax.broadcasted_iota(jnp.int32, (256, 256), 0)
        <= lax.broadcasted_iota(jnp.int32, (256, 256), 1)
    )
    upto = jnp.where(upto, 1.0, 0.0).astype(BF16)
    seen = jnp.zeros((DEV, 1), F32)
    for b in range(TILES // 2):
        block = chosen[:, 256 * b : 256 * (b + 1)]
        count = jnp.dot(block, upto, preferred_element_type=F32)
        place = jnp.sum(block.astype(F32) * (count + seen), axis=0, keepdims=True) - 1.0
        z_pos[2 * b : 2 * b + 1, :] = place[:, :128]
        z_pos[2 * b + 1 : 2 * b + 2, :] = place[:, 128:]
        seen = seen + count[:, 255:256]

    slot_row = lax.broadcasted_iota(jnp.int32, (HALF, 128), 0).astype(F32)

    def fill_slots(t, carry):
        columns = pl.ds(pl.multiple_of(t * 128, 128), 128)
        here = z_pos[pl.ds(t, 1), :] == slot_row
        for target, first, second in ((slot_a, 0, 2), (slot_b, 4, 6)):
            for piece in range(2):
                for rows_at, which in ((0, first), (HALF, second)):
                    value = z_val[which + piece, pl.ds(t, 1), :]
                    target[piece, rows_at : rows_at + HALF, columns] = jnp.where(
                        here, value, 0.0
                    ).astype(BF16)
        return carry

    lax.fori_loop(0, TILES, fill_slots, 0, unroll=2)
    for i, source in enumerate((slot_a, slot_b)):
        total = jnp.zeros((DEV, 128), F32)
        for piece in range(2):
            total = total + lax.dot_general(
                chosen[...], source[piece], (((1,), (1,)), ((), ())), preferred_element_type=F32
            )
        out_slots[i] = total

    def add_pressure(k, heavy):
        at = pl.multiple_of(k * 8, 8)
        temp, salt = st[pl.ds(at, 8), :], st[pl.ds(128 + at, 8), :]
        heavy = heavy + jnp.where(k < level, 0.8 * salt - 0.2 * temp, 0.0)
        pres[pl.ds(at, 8), :] = 0.1 * heavy
        return heavy

    lax.fori_loop(0, NZ, add_pressure, jnp.zeros((8, 128), F32), unroll=4)
    level_f = level.astype(F32)
    is_top = oy == N_OY - 1
    backward = 127 - lane
    for i in range(10):
        source, base = (st, 64 * i) if i < 8 else (pres, 64 * (i - 8))
        part = pl.ds(8 * i, 8)
        south_out[part, :] = source[pl.ds(base, 8, stride=8), :]
        top = source[pl.ds(base + 7, 8, stride=8), :]
        mirrored = jnp.take_along_axis(top, backward, axis=1)
        if 4 <= i < 8:
            mirrored = -mirrored
        north_out[part, :] = jnp.where(is_top, mirrored, top)
    top = jnp.broadcast_to(level_f[7:8, :], (8, 128))
    mirrored = jnp.take_along_axis(top, backward, axis=1)
    north_out[80:88, :] = jnp.where(is_top, mirrored, top)
    south_out[80:88, :] = jnp.broadcast_to(level_f[0:1, :], (8, 128))

    def pack_columns(k, packed):
        west, east = packed
        at = pl.multiple_of(k * 8, 8)
        for f in range(5):
            source, base = (st, 128 * f) if f < 4 else (pres, 0)
            plane = source[pl.ds(base + at, 8), :]
            place = 16 * f + k
            west = jnp.where(lane == place, pltpu.roll(plane, place, 1), west)
            east = jnp.where(lane == place, pltpu.roll(plane, place + 1, 1), east)
        return west, east

    none = jnp.zeros((8, 128), F32)
    west, east = lax.fori_loop(0, NZ, pack_columns, (none, none), unroll=2)
    west_out[...] = jnp.where(lane == 80, pltpu.roll(level_f, 80, 1), west)
    east_out[...] = jnp.where(lane == 80, pltpu.roll(level_f, 81, 1), east)

    pl.semaphore_wait(barrier, DEV - 1)
    for mask in SENDS:
        partner = me ^ mask
        pltpu.make_async_remote_copy(
            out_slots.at[:, pl.ds(partner, 1)], in_slots.at[:, pl.ds(me, 1)],
            out_sem.at[0], in_sem.at[0], device_id=partner, device_id_type=LOGICAL,
        ).start()
    own_slots = pltpu.make_async_copy(
        out_slots.at[:, pl.ds(me, 1)], in_slots.at[:, pl.ds(me, 1)], local_sem.at[0]
    )
    own_slots.start()

    def halo(source, target, out_at, in_at, device):
        return pltpu.make_async_remote_copy(
            source, target, halo_out_sem.at[out_at], halo_in_sem.at[in_at],
            device_id=device, device_id_type=LOGICAL,
        )

    to_west = halo(west_out, side_in.at[0], 2, 2, lax.rem(ox + n_ox - 1, n_ox) * N_OY + oy)
    to_east = halo(east_out, side_in.at[1], 3, 3, lax.rem(ox + 1, n_ox) * N_OY + oy)
    above = jnp.where(is_top, me ^ (DEV - N_OY), me + 1)
    lands = jnp.where(is_top, 0, 1)
    to_north = halo(north_out, halo_in.at[lands], 0, lands, above)
    to_south = halo(south_out, halo_in.at[0], 1, 0, me - 1)
    to_west.start()
    to_east.start()
    to_north.start()

    @pl.when(oy > 0)
    def _():
        to_south.start()

    def everything(buffers, which):
        source, target = buffers
        if which == 0:
            source, target = source.at[:, pl.ds(0, DEV - 1)], target.at[:, pl.ds(0, DEV - 1)]
        else:
            source, target = source.at[pl.ds(0, DEV - 1)], target.at[pl.ds(0, DEV - 1)]
        return pltpu.make_async_remote_copy(
            source, target, out_sem.at[which], in_sem.at[which],
            device_id=me ^ 1, device_id_type=LOGICAL,
        )

    slots_moved = everything((out_slots, in_slots), 0)
    slots_moved.wait_recv()
    own_slots.wait()

    for i in range(8):
        a, b = pl.ds(8 * i, 8), pl.ds(HALF + 8 * i, 8)
        for plane, first, second in ((0, 0, 2), (1, 4, None)):
            one, two = in_slots[plane, a, :], in_slots[plane, b, :]
            head = jnp.where(low_half, one, pltpu.roll(two, HALF, 1))
            tail = jnp.where(low_half, pltpu.roll(one, HALF, 1), two)
            rows[first, a, :], rows[first + 1, a, :] = split(head)
            if second is not None:
                rows[second, a, :], rows[second + 1, a, :] = split(tail)
            else:
                rows[6, a, :] = tail
    column_row = lax.broadcasted_iota(jnp.int32, (HALF, 128), 0)
    sums = jnp.zeros((48, HALF), F32)
    for start in range(0, HALF, GROUP):
        lefts, rights = [], []
        for r in range(start, start + GROUP):
            place = rows[6, r : r + 1, :].astype(jnp.int32)
            rights.append(jnp.where((place & 63) == column_row, 1.0, 0.0).astype(BF16))
            mine = (((place >> 7) & 3) + ((place >> 4) & 4)) == sub
            lefts.append(
                jnp.concatenate(
                    [jnp.where(mine, rows[i, r : r + 1, :], 0.0) for i in range(6)], axis=0
                ).astype(BF16)
            )
        sums = sums + lax.dot_general(
            jnp.concatenate(lefts, axis=1),
            jnp.concatenate(rights, axis=1),
            (((1,), (1,)), ((), ())),
            preferred_element_type=F32,
        )
    total_t, total_s, total_w = (
        jnp.concatenate([part, pltpu.roll(part, 4, 0)], axis=1)
        for part in (sums[16 * i : 16 * i + 8] + sums[16 * i + 8 : 16 * i + 16] for i in range(3))
    )
    divisor = jnp.maximum(total_w, 1.0)
    heat_flux = atm[1] * (atm[0] - total_t / divisor)
    fresh_flux = atm[2] * (total_s / divisor)
    for i in range(TILES // 2):
        a, b = pl.ds(8 * i, 8), pl.ds(HALF + 8 * i, 8)
        place = rows[6, a, :].astype(jnp.int32)
        column, chunk = place & 127, place >> 7
        heat, fresh = none, none
        for h in range(4):
            here = chunk == h
            table = jnp.broadcast_to(heat_flux[h : h + 1, :], (8, 128))
            heat = jnp.where(here, jnp.take_along_axis(table, column, axis=1), heat)
            table = jnp.broadcast_to(fresh_flux[h : h + 1, :], (8, 128))
            fresh = jnp.where(here, jnp.take_along_axis(table, column, axis=1), fresh)
        out_flux[a, :] = jnp.where(low_half, heat, pltpu.roll(fresh, HALF, 1))
        out_flux[b, :] = jnp.where(low_half, pltpu.roll(heat, HALF, 1), fresh)

    for mask in RETURNS:
        partner = me ^ mask
        pltpu.make_async_remote_copy(
            out_flux.at[pl.ds(partner, 1)], in_flux.at[pl.ds(me, 1)],
            out_sem.at[1], in_sem.at[1], device_id=partner, device_id_type=LOGICAL,
        ).start()
    own_flux = pltpu.make_async_copy(
        out_flux.at[pl.ds(me, 1)], in_flux.at[pl.ds(me, 1)], local_sem.at[1]
    )
    own_flux.start()

    halo(west_out, side_in.at[0], 2, 2, me).wait_recv()
    halo(east_out, side_in.at[1], 3, 3, me).wait_recv()
    halo(north_out, halo_in.at[0], 0, 0, me).wait_recv()

    @pl.when(oy > 0)
    def _():
        halo(north_out, halo_in.at[1], 0, 1, me).wait_recv()

    @pl.when(oy == 0)
    def _():
        halo_in[1] = jnp.zeros((PLANES, 128), F32)

    from_east, from_west = side_in[0], side_in[1]

    def around(plane, place):
        return (
            jnp.where(lane == 127, pltpu.roll(from_east, 127 - place, 1), pltpu.roll(plane, 127, 1)),
            jnp.where(lane == 0, pltpu.roll(from_west, (128 - place) & 127, 1), pltpu.roll(plane, 1, 1)),
            jnp.where(sub == 7, halo_in[0, pl.ds(place, 1), :], pltpu.roll(plane, 7, 0)),
            jnp.where(sub == 0, halo_in[1, pl.ds(place, 1), :], pltpu.roll(plane, 1, 0)),
        )

    levels_near = around(level_f, 80)
    row_at = (oy * CY + sub).astype(F32)
    coriolis = 0.2 + 0.8 * row_at / (CY * N_OY)

    def step(k, carry):
        depth = k.astype(F32)
        at = pl.multiple_of(k * 8, 8)
        up = pl.multiple_of(jnp.maximum(k - 1, 0) * 8, 8)
        down = pl.multiple_of(jnp.minimum(k + 1, NZ - 1) * 8, 8)
        wet = (depth < level_f).astype(F32)
        wet_near = [(depth < near).astype(F32) for near in levels_near]
        wet_down = jnp.where(k < NZ - 1, (depth + 1.0 < level_f).astype(F32), 0.0)
        wet_up = jnp.where(k > 0, (depth - 1.0 < level_f).astype(F32), 0.0)

        def spread(plane, place):
            total = none
            for near, mask in zip(around(plane, place), wet_near):
                total = total + mask * (near - plane)
            return wet * total

        for f in range(2):
            base = 128 * f
            plane = st[pl.ds(base + at, 8), :]
            over, under = st[pl.ds(base + up, 8), :], st[pl.ds(base + down, 8), :]
            vertical = wet * (wet_down * (under - plane) + wet_up * (over - plane))
            out[pl.ds(base + at, 8), :] = wet * (
                plane + EDDY_KAPPA * (spread(plane, 16 * f + k) + vertical)
            )
        p = pres[pl.ds(at, 8), :]
        p_e, p_w, p_n, p_s = around(p, 64 + k)
        grad_x = 0.5 * (wet_near[0] * (p_e - p) + wet_near[1] * (p - p_w))
        grad_y = 0.5 * (wet_near[2] * (p_n - p) + wet_near[3] * (p - p_s))
        u, v = st[pl.ds(256 + at, 8), :], st[pl.ds(384 + at, 8), :]
        out[pl.ds(256 + at, 8), :] = wet * (
            u + STEP * (coriolis * v - grad_x) + VISC * spread(u, 32 + k)
        )
        out[pl.ds(384 + at, 8), :] = wet * (
            v + STEP * (-coriolis * u - grad_y) + VISC * spread(v, 48 + k)
        )
        return carry

    lax.fori_loop(0, NZ, step, 0, unroll=2)

    flux_moved = everything((out_flux, in_flux), 1)
    flux_moved.wait_recv()
    own_flux.wait()

    flipped[...] = in_flux[...].T
    owners = [z_own[8 * c : 8 * c + 8, :] for c in range(2)]
    places = [z_pos[8 * c : 8 * c + 8, :] for c in range(2)]
    found = [[none, none], [none, none]]
    pieces = []
    for v in (1,):
        high, low = split(flipped[HALF * v : HALF * v + SLOTS, :])
        pieces += [high.astype(BF16), low.astype(BF16)]
    pieces = jnp.concatenate(pieces, axis=0)
    slot_at = lax.broadcasted_iota(jnp.int32, (SLOTS, 128), 0).astype(F32)
    for b in range(TILES // 2):
        near = jnp.dot(pieces, chosen[:, 256 * b : 256 * (b + 1)], preferred_element_type=F32)
        for half in range(2):
            t = 2 * b + half
            here = z_pos[t : t + 1, :] == slot_at
            columns = slice(128 * half, 128 * (half + 1))
            for i, v in enumerate((1,)):
                at = 2 * SLOTS * i
                both = near[at : at + SLOTS, columns] + near[at + SLOTS : at + 2 * SLOTS, columns]
                z_val[v, t : t + 1, :] = jnp.sum(
                    jnp.where(here, both, 0.0), axis=0, keepdims=True
                )
    for s in range(SLOTS):
        for c in range(2):
            here = places[c] == float(s)
            for v in (0,):
                table = jnp.broadcast_to(flipped[HALF * v + s : HALF * v + s + 1, :], (8, 128))
                found[v][c] = jnp.where(
                    here, jnp.take_along_axis(table, owners[c], axis=1), found[v][c]
                )
    for v in (1,):
        found[v] = [z_val[v, 8 * c : 8 * c + 8, :] for c in range(2)]
    area_0, area_1 = z_area[0:8, :], z_area[8:16, :]
    share = SEA_TOP * wet_top / (area_0 + area_1)
    for v in range(2):
        surface = (area_0 * found[v][0] + area_1 * found[v][1]) * share
        out[128 * v : 128 * v + 8, :] = out[128 * v : 128 * v + 8, :] + surface

    slots_moved.wait_send()
    flux_moved.wait_send()
    to_west.wait_send()
    to_east.wait_send()
    to_north.wait_send()

    @pl.when(oy > 0)
    def _():
        to_south.wait_send()


def per_device(state, levels, owner, atm_cell, area, air_temp, exchange_rate, rainfall):
    any_space = pl.BlockSpec(memory_space=pl.ANY)
    result = pl.pallas_call(
        kernel,
        out_shape=pltpu.VMEM((4 * NZ * CY, CX), F32),
        in_specs=[any_space] * 8,
        out_specs=pl.BlockSpec(memory_space=pltpu.VMEM),
        scratch_shapes=[
            pltpu.VMEM((512, 128), F32),
            pltpu.VMEM((8, 128), jnp.int32),
            pltpu.VMEM((TILES, 128), jnp.int32),
            pltpu.VMEM((TILES, 128), jnp.int32),
            pltpu.VMEM((TILES, 128), F32),
            pltpu.VMEM((3, 8, 128), F32),
            pltpu.VMEM((TILES, 128), jnp.int32),
            pltpu.VMEM((TILES, 128), jnp.int32),
            pltpu.VMEM((TILES, 128), F32),
            pltpu.VMEM((TILES, 128), F32),
            pltpu.VMEM((8, TILES, 128), F32),
            pltpu.VMEM((DEV, TILES * 128), BF16),
            pltpu.VMEM((2, 128, TILES * 128), BF16),
            pltpu.VMEM((2, 128, TILES * 128), BF16),
            pltpu.VMEM((2, DEV, 128), F32),
            pltpu.VMEM((2, DEV, 128), F32),
            pltpu.VMEM((DEV, 128), F32),
            pltpu.VMEM((DEV, 128), F32),
            pltpu.VMEM((128, 128), F32),
            pltpu.VMEM((7, HALF, 128), F32),
            pltpu.VMEM((128, 128), F32),
            pltpu.VMEM((PLANES, 128), F32),
            pltpu.VMEM((PLANES, 128), F32),
            pltpu.VMEM((2, PLANES, 128), F32),
            pltpu.VMEM((8, 128), F32),
            pltpu.VMEM((8, 128), F32),
            pltpu.VMEM((2, 8, 128), F32),
            pltpu.SemaphoreType.DMA((11,)),
            pltpu.SemaphoreType.DMA((2,)),
            pltpu.SemaphoreType.DMA((2,)),
            pltpu.SemaphoreType.DMA((4,)),
            pltpu.SemaphoreType.DMA((4,)),
        ],
        compiler_params=pltpu.CompilerParams(
            collective_id=0, has_side_effects=True, vmem_limit_bytes=56 * 1024 * 1024
        ),
    )(
        state.reshape(4 * NZ * CY, CX),
        levels,
        owner.reshape(TILES, 128),
        atm_cell.reshape(TILES, 128),
        area.reshape(TILES, 128),
        air_temp.reshape(4, 128),
        exchange_rate.reshape(4, 128),
        rainfall.reshape(4, 128),
    )
    return result.reshape(4, NZ, CY, CX)


def solution(mesh):
    entries = P(("ox", "oy"))
    in_specs = (
        P(None, None, "oy", "ox"),
        P("oy", "ox"),
        P(("ox", "oy"), None),
        entries,
        entries,
        entries,
        entries,
        entries,
    )
    return jax.shard_map(
        per_device,
        mesh=mesh,
        in_specs=in_specs,
        out_specs=P(None, None, "oy", "ox"),
        check_vma=False,
    )
```

```python
import jax
import jax.numpy as jnp
from jax import lax
from jax.experimental import pallas as pl
from jax.experimental.pallas import tpu as pltpu
from jax.sharding import PartitionSpec as P

NZ = 16
CY = 8
CX = 128
DEV = 128
N_OY = 4
TILES = 16
HALF = 64
SLOTS = 48
GROUP = 8
PLANES = 88
EDDY_KAPPA = 0.1
VISC = 0.1
STEP = 0.2
SEA_TOP = 0.5
F32 = jnp.float32
BF16 = jnp.bfloat16
LOGICAL = pl.DeviceIdType.LOGICAL


def hops(mask):
    ring = (0, 1, 2, 1)
    return 4 * (ring[mask & 3] + ring[(mask >> 3) & 3] + ring[(mask >> 5) & 3]) + ((mask >> 2) & 1)


PARTNERS = sorted(range(1, DEV), key=lambda mask: -(hops(mask) // 4))
SENDS = sorted(range(DEV - 1, 0, -1), key=lambda mask: -(hops(mask) // 4))
RETURNS = sorted(range(DEV - 1, 0, -1), key=lambda mask: -(hops(mask) // 4))


def split(value):
    high = value.astype(BF16).astype(F32)
    return high, value - high


def kernel(
    state, levels, owner, cell, area, air, rate, rain,
    out,
    st, lev, raw_own, raw_cell, raw_area, atm,
    z_own, z_cell, z_pos, z_area, z_val,
    chosen, slot_a, slot_b,
    out_slots, in_slots, out_flux, in_flux, flipped,
    rows,
    pres, north_out, south_out, halo_in, west_out, east_out, side_in,
    local_sem, out_sem, in_sem, halo_out_sem, halo_in_sem,
):
    ox, oy = lax.axis_index("ox"), lax.axis_index("oy")
    me = ox * N_OY + oy
    n_ox = DEV // N_OY

    loads = [
        pltpu.make_async_copy(source, target, local_sem.at[i])
        for i, (source, target) in enumerate(
            (
                (owner, raw_own), (cell, raw_cell), (area, raw_area), (levels, lev), (state, st),
                (air, atm.at[0, 0:4]), (air, atm.at[0, 4:8]),
                (rate, atm.at[1, 0:4]), (rate, atm.at[1, 4:8]),
                (rain, atm.at[2, 0:4]), (rain, atm.at[2, 4:8]),
            )
        )
    ]
    barrier = pltpu.get_barrier_semaphore()
    for mask in PARTNERS[:44]:
        pl.semaphore_signal(barrier, inc=1, device_id=me ^ mask, device_id_type=LOGICAL)
    for copy in loads:
        copy.start()
    for mask in PARTNERS[44:]:
        pl.semaphore_signal(barrier, inc=1, device_id=me ^ mask, device_id_type=LOGICAL)
    for copy in loads:
        copy.wait()

    lane = lax.broadcasted_iota(jnp.int32, (8, 128), 1)
    sub = lax.broadcasted_iota(jnp.int32, (8, 128), 0)
    low_half = lane < HALF
    level = lev[...]

    for source, target in ((raw_own, z_own), (raw_cell, z_cell), (raw_area, z_area)):
        even, odd = source[pl.ds(0, 8, stride=2), :], source[pl.ds(1, 8, stride=2), :]
        for c in range(2):
            index = 2 * (lane & (HALF - 1)) + c
            target[pl.ds(8 * c, 8), :] = jnp.where(
                low_half,
                jnp.take_along_axis(even, index, axis=1),
                jnp.take_along_axis(odd, index, axis=1),
            )
    wet_top = (level > 0).astype(F32)
    temp_top, salt_top = st[0:8, :], st[128:136, :]
    for c in range(2):
        part = pl.ds(8 * c, 8)
        weight = z_area[part, :] * wet_top
        for i, value in enumerate(
            (weight * temp_top, weight * salt_top, weight, z_cell[part, :].astype(F32))
        ):
            high, low = split(value)
            z_val[2 * i, part, :] = high
            z_val[2 * i + 1, part, :] = low

    owner_row = lax.broadcasted_iota(jnp.int32, (DEV, 128), 0)

    def mark_owner(t, carry):
        columns = pl.ds(pl.multiple_of(t * 128, 128), 128)
        chosen[:, columns] = jnp.where(z_own[pl.ds(t, 1), :] == owner_row, 1.0, 0.0).astype(BF16)
        return carry

    lax.fori_loop(0, TILES, mark_owner, 0, unroll=4)

    upto = (
        lax.broadcasted_iota(jnp.int32, (256, 256), 0)
        <= lax.broadcasted_iota(jnp.int32, (256, 256), 1)
    )
    upto = jnp.where(upto, 1.0, 0.0).astype(BF16)
    seen = jnp.zeros((DEV, 1), F32)
    for b in range(TILES // 2):
        block = chosen[:, 256 * b : 256 * (b + 1)]
        count = jnp.dot(block, upto, preferred_element_type=F32)
        place = jnp.sum(block.astype(F32) * (count + seen), axis=0, keepdims=True) - 1.0
        z_pos[2 * b : 2 * b + 1, :] = place[:, :128]
        z_pos[2 * b + 1 : 2 * b + 2, :] = place[:, 128:]
        seen = seen + count[:, 255:256]

    slot_row = lax.broadcasted_iota(jnp.int32, (HALF, 128), 0).astype(F32)

    def fill_slots(t, carry):
        columns = pl.ds(pl.multiple_of(t * 128, 128), 128)
        here = z_pos[pl.ds(t, 1), :] == slot_row
        for target, first, second in ((slot_a, 0, 2), (slot_b, 4, 6)):
            for piece in range(2):
                for rows_at, which in ((0, first), (HALF, second)):
                    value = z_val[which + piece, pl.ds(t, 1), :]
                    target[piece, rows_at : rows_at + HALF, columns] = jnp.where(
                        here, value, 0.0
                    ).astype(BF16)
        return carry

    lax.fori_loop(0, TILES, fill_slots, 0, unroll=2)
    for i, source in enumerate((slot_a, slot_b)):
        total = jnp.zeros((DEV, 128), F32)
        for piece in range(2):
            total = total + lax.dot_general(
                chosen[...], source[piece], (((1,), (1,)), ((), ())), preferred_element_type=F32
            )
        out_slots[i] = total

    pl.semaphore_wait(barrier, DEV - 1)
    for mask in SENDS:
        partner = me ^ mask
        pltpu.make_async_remote_copy(
            out_slots.at[:, pl.ds(partner, 1)], in_slots.at[:, pl.ds(me, 1)],
            out_sem.at[0], in_sem.at[0], device_id=partner, device_id_type=LOGICAL,
        ).start()
    own_slots = pltpu.make_async_copy(
        out_slots.at[:, pl.ds(me, 1)], in_slots.at[:, pl.ds(me, 1)], local_sem.at[0]
    )
    own_slots.start()

    def add_pressure(k, heavy):
        at = pl.multiple_of(k * 8, 8)
        temp, salt = st[pl.ds(at, 8), :], st[pl.ds(128 + at, 8), :]
        heavy = heavy + jnp.where(k < level, 0.8 * salt - 0.2 * temp, 0.0)
        pres[pl.ds(at, 8), :] = 0.1 * heavy
        return heavy

    lax.fori_loop(0, NZ, add_pressure, jnp.zeros((8, 128), F32), unroll=4)
    level_f = level.astype(F32)
    is_top = oy == N_OY - 1
    backward = 127 - lane
    for i in range(10):
        source, base = (st, 64 * i) if i < 8 else (pres, 64 * (i - 8))
        part = pl.ds(8 * i, 8)
        south_out[part, :] = source[pl.ds(base, 8, stride=8), :]
        top = source[pl.ds(base + 7, 8, stride=8), :]
        mirrored = jnp.take_along_axis(top, backward, axis=1)
        if 4 <= i < 8:
            mirrored = -mirrored
        north_out[part, :] = jnp.where(is_top, mirrored, top)
    top = jnp.broadcast_to(level_f[7:8, :], (8, 128))
    mirrored = jnp.take_along_axis(top, backward, axis=1)
    north_out[80:88, :] = jnp.where(is_top, mirrored, top)
    south_out[80:88, :] = jnp.broadcast_to(level_f[0:1, :], (8, 128))

    def pack_columns(k, packed):
        west, east = packed
        at = pl.multiple_of(k * 8, 8)
        for f in range(5):
            source, base = (st, 128 * f) if f < 4 else (pres, 0)
            plane = source[pl.ds(base + at, 8), :]
            place = 16 * f + k
            west = jnp.where(lane == place, pltpu.roll(plane, place, 1), west)
            east = jnp.where(lane == place, pltpu.roll(plane, place + 1, 1), east)
        return west, east

    none = jnp.zeros((8, 128), F32)
    west, east = lax.fori_loop(0, NZ, pack_columns, (none, none), unroll=2)
    west_out[...] = jnp.where(lane == 80, pltpu.roll(level_f, 80, 1), west)
    east_out[...] = jnp.where(lane == 80, pltpu.roll(level_f, 81, 1), east)

    def halo(source, target, out_at, in_at, device):
        return pltpu.make_async_remote_copy(
            source, target, halo_out_sem.at[out_at], halo_in_sem.at[in_at],
            device_id=device, device_id_type=LOGICAL,
        )

    to_west = halo(west_out, side_in.at[0], 2, 2, lax.rem(ox + n_ox - 1, n_ox) * N_OY + oy)
    to_east = halo(east_out, side_in.at[1], 3, 3, lax.rem(ox + 1, n_ox) * N_OY + oy)
    above = jnp.where(is_top, me ^ (DEV - N_OY), me + 1)
    lands = jnp.where(is_top, 0, 1)
    to_north = halo(north_out, halo_in.at[lands], 0, lands, above)
    to_south = halo(south_out, halo_in.at[0], 1, 0, me - 1)
    to_west.start()
    to_east.start()
    to_north.start()

    @pl.when(oy > 0)
    def _():
        to_south.start()

    def everything(buffers, which):
        source, target = buffers
        if which == 0:
            source, target = source.at[:, pl.ds(0, DEV - 1)], target.at[:, pl.ds(0, DEV - 1)]
        else:
            source, target = source.at[pl.ds(0, DEV - 1)], target.at[pl.ds(0, DEV - 1)]
        return pltpu.make_async_remote_copy(
            source, target, out_sem.at[which], in_sem.at[which],
            device_id=me ^ 1, device_id_type=LOGICAL,
        )

    slots_moved = everything((out_slots, in_slots), 0)
    slots_moved.wait_recv()
    own_slots.wait()

    for i in range(8):
        a, b = pl.ds(8 * i, 8), pl.ds(HALF + 8 * i, 8)
        for plane, first, second in ((0, 0, 2), (1, 4, None)):
            one, two = in_slots[plane, a, :], in_slots[plane, b, :]
            head = jnp.where(low_half, one, pltpu.roll(two, HALF, 1))
            tail = jnp.where(low_half, pltpu.roll(one, HALF, 1), two)
            rows[first, a, :], rows[first + 1, a, :] = split(head)
            if second is not None:
                rows[second, a, :], rows[second + 1, a, :] = split(tail)
            else:
                rows[6, a, :] = tail
    column_row = lax.broadcasted_iota(jnp.int32, (HALF, 128), 0).astype(F32).astype(BF16)
    one, zero = jnp.ones((HALF, 128), BF16), jnp.zeros((HALF, 128), BF16)
    sums = jnp.zeros((48, HALF), F32)
    for start in range(0, HALF, GROUP):
        lefts, rights = [], []
        for r in range(start, start + GROUP):
            place = rows[6, r : r + 1, :].astype(jnp.int32)
            column = (place & 63).astype(F32).astype(BF16)
            rights.append(jnp.where(column == column_row, one, zero))
            mine = (((place >> 7) & 3) + ((place >> 4) & 4)) == sub
            lefts.append(
                jnp.concatenate(
                    [jnp.where(mine, rows[i, r : r + 1, :], 0.0) for i in range(6)], axis=0
                ).astype(BF16)
            )
        sums = sums + lax.dot_general(
            jnp.concatenate(lefts, axis=1),
            jnp.concatenate(rights, axis=1),
            (((1,), (1,)), ((), ())),
            preferred_element_type=F32,
        )
    total_t, total_s, total_w = (
        jnp.concatenate([part, pltpu.roll(part, 4, 0)], axis=1)
        for part in (sums[16 * i : 16 * i + 8] + sums[16 * i + 8 : 16 * i + 16] for i in range(3))
    )
    divisor = jnp.maximum(total_w, 1.0)
    heat_flux = atm[1] * (atm[0] - total_t / divisor)
    fresh_flux = atm[2] * (total_s / divisor)
    for i in range(TILES // 2):
        a, b = pl.ds(8 * i, 8), pl.ds(HALF + 8 * i, 8)
        place = rows[6, a, :].astype(jnp.int32)
        column, chunk = place & 127, place >> 7
        heat, fresh = none, none
        for h in range(4):
            here = chunk == h
            table = jnp.broadcast_to(heat_flux[h : h + 1, :], (8, 128))
            heat = jnp.where(here, jnp.take_along_axis(table, column, axis=1), heat)
            table = jnp.broadcast_to(fresh_flux[h : h + 1, :], (8, 128))
            fresh = jnp.where(here, jnp.take_along_axis(table, column, axis=1), fresh)
        out_flux[a, :] = jnp.where(low_half, heat, pltpu.roll(fresh, HALF, 1))
        out_flux[b, :] = jnp.where(low_half, pltpu.roll(heat, HALF, 1), fresh)

    for mask in RETURNS:
        partner = me ^ mask
        pltpu.make_async_remote_copy(
            out_flux.at[pl.ds(partner, 1)], in_flux.at[pl.ds(me, 1)],
            out_sem.at[1], in_sem.at[1], device_id=partner, device_id_type=LOGICAL,
        ).start()
    own_flux = pltpu.make_async_copy(
        out_flux.at[pl.ds(me, 1)], in_flux.at[pl.ds(me, 1)], local_sem.at[1]
    )
    own_flux.start()

    halo(west_out, side_in.at[0], 2, 2, me).wait_recv()
    halo(east_out, side_in.at[1], 3, 3, me).wait_recv()
    halo(north_out, halo_in.at[0], 0, 0, me).wait_recv()

    @pl.when(oy > 0)
    def _():
        halo(north_out, halo_in.at[1], 0, 1, me).wait_recv()

    @pl.when(oy == 0)
    def _():
        halo_in[1] = jnp.zeros((PLANES, 128), F32)

    from_east, from_west = side_in[0], side_in[1]

    def around(plane, place):
        return (
            jnp.where(lane == 127, pltpu.roll(from_east, 127 - place, 1), pltpu.roll(plane, 127, 1)),
            jnp.where(lane == 0, pltpu.roll(from_west, (128 - place) & 127, 1), pltpu.roll(plane, 1, 1)),
            jnp.where(sub == 7, halo_in[0, pl.ds(place, 1), :], pltpu.roll(plane, 7, 0)),
            jnp.where(sub == 0, halo_in[1, pl.ds(place, 1), :], pltpu.roll(plane, 1, 0)),
        )

    levels_near = around(level_f, 80)
    row_at = (oy * CY + sub).astype(F32)
    coriolis = 0.2 + 0.8 * row_at / (CY * N_OY)

    def step(k, carry):
        depth = k.astype(F32)
        at = pl.multiple_of(k * 8, 8)
        up = pl.multiple_of(jnp.maximum(k - 1, 0) * 8, 8)
        down = pl.multiple_of(jnp.minimum(k + 1, NZ - 1) * 8, 8)
        wet = (depth < level_f).astype(F32)
        wet_near = [(depth < near).astype(F32) for near in levels_near]
        wet_down = jnp.where(k < NZ - 1, (depth + 1.0 < level_f).astype(F32), 0.0)
        wet_up = jnp.where(k > 0, (depth - 1.0 < level_f).astype(F32), 0.0)

        def spread(plane, place):
            total = none
            for near, mask in zip(around(plane, place), wet_near):
                total = total + mask * (near - plane)
            return wet * total

        for f in range(2):
            base = 128 * f
            plane = st[pl.ds(base + at, 8), :]
            over, under = st[pl.ds(base + up, 8), :], st[pl.ds(base + down, 8), :]
            vertical = wet * (wet_down * (under - plane) + wet_up * (over - plane))
            out[pl.ds(base + at, 8), :] = wet * (
                plane + EDDY_KAPPA * (spread(plane, 16 * f + k) + vertical)
            )
        p = pres[pl.ds(at, 8), :]
        p_e, p_w, p_n, p_s = around(p, 64 + k)
        grad_x = 0.5 * (wet_near[0] * (p_e - p) + wet_near[1] * (p - p_w))
        grad_y = 0.5 * (wet_near[2] * (p_n - p) + wet_near[3] * (p - p_s))
        u, v = st[pl.ds(256 + at, 8), :], st[pl.ds(384 + at, 8), :]
        out[pl.ds(256 + at, 8), :] = wet * (
            u + STEP * (coriolis * v - grad_x) + VISC * spread(u, 32 + k)
        )
        out[pl.ds(384 + at, 8), :] = wet * (
            v + STEP * (-coriolis * u - grad_y) + VISC * spread(v, 48 + k)
        )
        return carry

    lax.fori_loop(0, NZ, step, 0, unroll=2)

    flux_moved = everything((out_flux, in_flux), 1)
    flux_moved.wait_recv()
    own_flux.wait()

    flipped[...] = in_flux[...].T
    owners = [z_own[8 * c : 8 * c + 8, :] for c in range(2)]
    places = [z_pos[8 * c : 8 * c + 8, :] for c in range(2)]
    found = [[none, none], [none, none]]
    pieces = []
    for v in (1,):
        high, low = split(flipped[HALF * v : HALF * v + SLOTS, :])
        pieces += [high.astype(BF16), low.astype(BF16)]
    pieces = jnp.concatenate(pieces, axis=0)
    slot_at = lax.broadcasted_iota(jnp.int32, (SLOTS, 128), 0).astype(F32)
    for b in range(TILES // 2):
        near = jnp.dot(pieces, chosen[:, 256 * b : 256 * (b + 1)], preferred_element_type=F32)
        for half in range(2):
            t = 2 * b + half
            here = z_pos[t : t + 1, :] == slot_at
            columns = slice(128 * half, 128 * (half + 1))
            for i, v in enumerate((1,)):
                at = 2 * SLOTS * i
                both = near[at : at + SLOTS, columns] + near[at + SLOTS : at + 2 * SLOTS, columns]
                z_val[v, t : t + 1, :] = jnp.sum(
                    jnp.where(here, both, 0.0), axis=0, keepdims=True
                )
    for s in range(SLOTS):
        for c in range(2):
            here = places[c] == float(s)
            for v in (0,):
                table = jnp.broadcast_to(flipped[HALF * v + s : HALF * v + s + 1, :], (8, 128))
                found[v][c] = jnp.where(
                    here, jnp.take_along_axis(table, owners[c], axis=1), found[v][c]
                )
    for v in (1,):
        found[v] = [z_val[v, 8 * c : 8 * c + 8, :] for c in range(2)]
    area_0, area_1 = z_area[0:8, :], z_area[8:16, :]
    share = SEA_TOP * wet_top / (area_0 + area_1)
    for v in range(2):
        surface = (area_0 * found[v][0] + area_1 * found[v][1]) * share
        out[128 * v : 128 * v + 8, :] = out[128 * v : 128 * v + 8, :] + surface

    slots_moved.wait_send()
    flux_moved.wait_send()
    to_west.wait_send()
    to_east.wait_send()
    to_north.wait_send()

    @pl.when(oy > 0)
    def _():
        to_south.wait_send()


def per_device(state, levels, owner, atm_cell, area, air_temp, exchange_rate, rainfall):
    any_space = pl.BlockSpec(memory_space=pl.ANY)
    result = pl.pallas_call(
        kernel,
        out_shape=pltpu.VMEM((4 * NZ * CY, CX), F32),
        in_specs=[any_space] * 8,
        out_specs=pl.BlockSpec(memory_space=pltpu.VMEM),
        scratch_shapes=[
            pltpu.VMEM((512, 128), F32),
            pltpu.VMEM((8, 128), jnp.int32),
            pltpu.VMEM((TILES, 128), jnp.int32),
            pltpu.VMEM((TILES, 128), jnp.int32),
            pltpu.VMEM((TILES, 128), F32),
            pltpu.VMEM((3, 8, 128), F32),
            pltpu.VMEM((TILES, 128), jnp.int32),
            pltpu.VMEM((TILES, 128), jnp.int32),
            pltpu.VMEM((TILES, 128), F32),
            pltpu.VMEM((TILES, 128), F32),
            pltpu.VMEM((8, TILES, 128), F32),
            pltpu.VMEM((DEV, TILES * 128), BF16),
            pltpu.VMEM((2, 128, TILES * 128), BF16),
            pltpu.VMEM((2, 128, TILES * 128), BF16),
            pltpu.VMEM((2, DEV, 128), F32),
            pltpu.VMEM((2, DEV, 128), F32),
            pltpu.VMEM((DEV, 128), F32),
            pltpu.VMEM((DEV, 128), F32),
            pltpu.VMEM((128, 128), F32),
            pltpu.VMEM((7, HALF, 128), F32),
            pltpu.VMEM((128, 128), F32),
            pltpu.VMEM((PLANES, 128), F32),
            pltpu.VMEM((PLANES, 128), F32),
            pltpu.VMEM((2, PLANES, 128), F32),
            pltpu.VMEM((8, 128), F32),
            pltpu.VMEM((8, 128), F32),
            pltpu.VMEM((2, 8, 128), F32),
            pltpu.SemaphoreType.DMA((11,)),
            pltpu.SemaphoreType.DMA((2,)),
            pltpu.SemaphoreType.DMA((2,)),
            pltpu.SemaphoreType.DMA((4,)),
            pltpu.SemaphoreType.DMA((4,)),
        ],
        compiler_params=pltpu.CompilerParams(
            collective_id=0, has_side_effects=True, vmem_limit_bytes=56 * 1024 * 1024
        ),
    )(
        state.reshape(4 * NZ * CY, CX),
        levels,
        owner.reshape(TILES, 128),
        atm_cell.reshape(TILES, 128),
        area.reshape(TILES, 128),
        air_temp.reshape(4, 128),
        exchange_rate.reshape(4, 128),
        rainfall.reshape(4, 128),
    )
    return result.reshape(4, NZ, CY, CX)


def solution(mesh):
    entries = P(("ox", "oy"))
    in_specs = (
        P(None, None, "oy", "ox"),
        P("oy", "ox"),
        P(("ox", "oy"), None),
        entries,
        entries,
        entries,
        entries,
        entries,
    )
    return jax.shard_map(
        per_device,
        mesh=mesh,
        in_specs=in_specs,
        out_specs=P(None, None, "oy", "ox"),
        check_vma=False,
    )
```
